512 devices in a mesh: dp: 32 (over y, z_lo, core), mp: 16 (over x, z_hi).
Axes of the slice: x: 4, y: 8, z: 8 (z_hi: 4, z_lo: 2; z = z_hi * 2 + z_lo), core: 2. Of those that a mesh axis runs over, the one named last changes fastest.
Arguments:
- activations: bfloat16 [32768, 4096], P('dp', 'mp'), may hold values from -6 to 6
- output_gradient_rows: bfloat16 [32768, 4096], P('dp', 'mp'), may hold values from -6 to 6
- adapter_up_matrix: bfloat16 [4096, 128], P('mp'), may hold values from -0.09375 to 0.09375
- rank_factor_signs: int32 [64, 128], replicated, may hold values from 0 to 65535
- feature_factor_signs: int32 [64, 4096], P(None, 'mp'), may hold values from 0 to 65535
- lengths: int32 [1024], P('dp'), may hold values from 1 to 32, 16384 in all
Outputs:
- sketches: bfloat16 [1024, 1024], P(('dp', 'mp'))
- cosines: float32 [1024, 32, 32], P('dp', None, 'mp')
The draws below stay inside these ranges and needn't reach their ends.
Inputs may be any that keep to these rules, and one draw needn't show every extreme that they name: `lengths`: every example has at least one live token and some example fills all 32 slots.
All inputs are finite; a program needn't handle non-finite values. No bound on the sum of `lengths` on one device may be relied on, other than what follows from the above.
Results may differ from the reference program's by a relative error of at most 0.004.
Values may be sent and summed in bfloat16 or wider, within the bound.
A program may use at most 64 MiB of HBM per device.

```python
import math
import jax
import jax.numpy as jnp
import numpy as np
from jax import lax

MODEL_WIDTH = 4096
ADAPTER_RANK = 128
K = 1024
EX_DEV = 32
SEQ = 32
EXAMPLES = 1024
TOKENS = 32768
WORDS = 64
N_DP = 32


def with_ends(values, rng, smallest, high):
    longest = values.shape.index(max(values.shape))
    spots = []
    for shift in (0, 1):
        where = [jax.random.randint(jax.random.fold_in(rng, axis), (), 0, length) for axis, length in enumerate(values.shape)]
        where[longest] = (where[longest] + shift) % values.shape[longest]
        spots.append(tuple(where))
    return values.at[spots[0]].set(smallest).at[spots[1]].set(high)


def block_scale(rng, extent, cuts, least, largest):
    loudness, own = 1.0, jax.random.fold_in(rng, 6)
    for axis_at, parts in cuts:
        draws = jnp.exp(jax.random.uniform(jax.random.fold_in(own, axis_at), (parts,), jnp.float32, least / len(cuts), largest / len(cuts)))
        loudness = loudness * jnp.repeat(draws, extent[axis_at] // parts).reshape([-1 if axis == axis_at else 1 for axis in range(len(extent))])
    return loudness


def profile(number_of, total, most, lean):
    loads = [(1 << 20) // math.isqrt(standing ** lean) + 1 for standing in range(2, number_of + 1)]
    rest, counts = total - most - (number_of - 1), [1] * (number_of - 1)
    while rest > 0:
        movable = [i for i in range(number_of - 1) if counts[i] < most]
        whole, budget = sum([loads[i] for i in movable]), rest
        for i in movable:
            addition = min(most - counts[i], max(1, budget * loads[i] // whole), rest)
            counts[i] = counts[i] + addition
            rest = rest - addition
    return np.array([most] + counts)


def uneven_parts(rng, number_of, total, limit, skew):
    if number_of == 2:
        one = jax.random.randint(rng, (), max(1, total - limit), min(limit, total - 1) + 1)
        return jnp.stack([one, total - one])
    sizes = jnp.asarray(profile(number_of, total, limit, skew), jnp.int32)
    couples = (number_of - 1) // 2
    donor, sink = sizes[1:1 + 2 * couples:2], sizes[2:2 + 2 * couples:2]
    margin = jnp.minimum(donor - 1, limit - sink)
    passed = jax.random.randint(jax.random.fold_in(rng, 1), (couples,), 0, 1 << 20) % (margin + 1)
    sizes = sizes.at[1:1 + 2 * couples:2].set(donor - passed).at[2:2 + 2 * couples:2].set(sink + passed)
    return sizes[jax.random.permutation(jax.random.fold_in(rng, 2), number_of)]


def normal_values(own_key, dims, deviation, reach, split=(), held_as=jnp.bfloat16):
    level = block_scale(own_key, dims, split, -0.22, 0.18) if split else 1.0
    drawn = jax.random.normal(own_key, dims, jnp.float32) * deviation * level
    return jnp.minimum(jnp.maximum(drawn, -reach), reach).astype(held_as)


def setup_inputs(seed: int = 0) -> dict:
    keys = jax.random.split(jax.random.key(seed), 7)
    activations = normal_values(keys[0], (TOKENS, MODEL_WIDTH), 1.0, 6.0, ((0, 32), (1, 16)))
    output_gradient_rows = normal_values(keys[1], (TOKENS, MODEL_WIDTH), 1.0, 6.0, ((0, 32), (1, 16)))
    adapter_up_matrix = normal_values(keys[2], (MODEL_WIDTH, ADAPTER_RANK), MODEL_WIDTH ** -0.5, 0.09375, ((0, 16),))
    rank_factor_signs = with_ends(jax.random.randint(keys[3], (WORDS, ADAPTER_RANK), 0, 65536), jax.random.fold_in(keys[3], 1), 0, 65535).astype(jnp.int32)
    feature_factor_signs = with_ends(jax.random.randint(keys[4], (WORDS, MODEL_WIDTH), 0, 65536), jax.random.fold_in(keys[4], 1), 0, 65535).astype(jnp.int32)
    lengths = uneven_parts(keys[5], EXAMPLES, EXAMPLES * SEQ // 2, SEQ, 1).astype(jnp.int32)
    return dict(activations=activations, output_gradient_rows=output_gradient_rows, adapter_up_matrix=adapter_up_matrix, rank_factor_signs=rank_factor_signs, feature_factor_signs=feature_factor_signs, lengths=lengths)


def unpack_signs(packed):
    offsets = jnp.arange(16, dtype=jnp.int32)
    bit_values = jnp.bitwise_and(jnp.right_shift(packed[:, None, :], offsets[None, :, None]), 1)
    return (2 * bit_values - 1).reshape(packed.shape[0] * 16, packed.shape[1]).astype(jnp.bfloat16)

def reference(activations, output_gradient_rows, adapter_up_matrix, rank_factor_signs, feature_factor_signs, lengths):
    slot_index = jnp.arange(TOKENS, dtype=jnp.int32)
    active_mask = (slot_index % SEQ < jnp.repeat(lengths, SEQ)).astype(jnp.float32)
    rank_gradient = jnp.dot(output_gradient_rows, adapter_up_matrix, preferred_element_type=jnp.float32) * active_mask[:, None]
    sign_rank = unpack_signs(rank_factor_signs).astype(jnp.float32)
    sign_feat = unpack_signs(feature_factor_signs)
    left_proj = jnp.dot(rank_gradient, sign_rank.T, precision=lax.Precision.HIGHEST)
    right_proj = jnp.dot(activations, sign_feat.T, preferred_element_type=jnp.float32)
    raw_sum = (left_proj * right_proj).reshape(EXAMPLES, SEQ, K).sum(axis=1)
    scaled = raw_sum * lax.rsqrt(lax.optimization_barrier(jnp.mean(raw_sum * raw_sum, axis=1, keepdims=True)) + 1e-06)
    sketches = scaled.astype(jnp.bfloat16)
    cos_full = jnp.dot(sketches, sketches.T, preferred_element_type=jnp.float32) / K
    return (sketches, cos_full.reshape(EXAMPLES, N_DP, EX_DEV))
```

```python
import functools

import jax
import jax.numpy as jnp
from jax import lax
from jax.experimental import pallas as pl
from jax.experimental.pallas import tpu as pltpu
from jax.sharding import PartitionSpec as P

MESH = pl.DeviceIdType.MESH
NT = (((1,), (1,)), ((), ()))
LANES = 128


def unpack_signs(words):
    shape = (words.shape[0], 16, words.shape[1])
    offsets = lax.broadcasted_iota(jnp.int32, shape, 1)
    bits = jnp.bitwise_and(jnp.right_shift(words[:, None, :], offsets), 1)
    signs = (2 * bits - 1).astype(jnp.float32).astype(jnp.bfloat16)
    return signs.reshape(shape[0] * 16, shape[2])


def kernel(
    n_dp, n_mp, seq,
    act_hbm, grad_hbm, up_hbm, rank_words_hbm, feat_words_hbm, lengths,
    sketch_out, cos_out,
    act, grad, up, rank_words, feat_words, in_sem,
    sign_rank, sign_feat, right,
    part, part_in, rank_sum, raw, raw_in, mine, group, others, group_f, others_f,
    part_send, part_recv, rank_send, rank_recv, raw_send, raw_recv,
    group_send, group_recv, other_send, other_recv,
):
    my_dp = lax.axis_index("dp")
    me = lax.axis_index("mp")
    rows = act.shape[0] // n_mp
    own = rows // seq
    blocks = sign_feat.shape[0] // LANES
    width = own * blocks

    loads = [
        pltpu.make_async_copy(src, dst, in_sem.at[at])
        for at, (src, dst) in enumerate(
            [
                (up_hbm, up),
                (grad_hbm, grad),
                (feat_words_hbm, feat_words),
                (act_hbm, act),
                (rank_words_hbm, rank_words),
            ]
        )
    ]
    for load in loads:
        load.start()

    barrier = pltpu.get_barrier_semaphore()

    @pl.loop(1, n_mp)
    def _(step):
        pl.semaphore_signal(
            barrier, inc=1, device_id=(my_dp, lax.rem(me + step, n_mp)), device_id_type=MESH
        )

    @pl.loop(1, n_dp)
    def _(step):
        pl.semaphore_signal(
            barrier, inc=1, device_id=(lax.rem(my_dp + step, n_dp), me), device_id_type=MESH
        )

    loads[0].wait()
    loads[1].wait()
    pl.semaphore_wait(barrier, n_mp + n_dp - 2)

    def send_part(to):
        return pltpu.make_async_remote_copy(
            src_ref=part.at[to], dst_ref=part_in.at[me],
            send_sem=part_send.at[to], recv_sem=part_recv.at[me],
            device_id=(my_dp, to), device_id_type=MESH,
        )

    def from_part(source):
        return pltpu.make_async_remote_copy(
            src_ref=part.at[source], dst_ref=part_in.at[source],
            send_sem=part_send.at[source], recv_sem=part_recv.at[source],
            device_id=(my_dp, source), device_id_type=MESH,
        )

    @pl.loop(1, n_mp + 1)
    def _(step):
        to = lax.rem(me + step, n_mp)
        tokens = grad[pl.ds(pl.multiple_of(to * rows, rows), rows), :]
        part[to] = jnp.dot(tokens, up[...], preferred_element_type=jnp.float32).astype(jnp.bfloat16)

        @pl.when(step < n_mp)
        def _():
            send_part(to).start()

    for load in loads[2:]:
        load.wait()
    sign_feat[...] = unpack_signs(feat_words[...])
    sign_rank[...] = unpack_signs(rank_words[...])

    @pl.loop(0, 4)
    def _(step):
        at = pl.ds(pl.multiple_of(step * (act.shape[0] // 4), act.shape[0] // 4), act.shape[0] // 4)
        right[at, :] = lax.dot_general(
            act[at, :], sign_feat[...], NT, preferred_element_type=jnp.float32
        )

    part_in[me] = part[me]

    @pl.loop(1, n_mp)
    def _(step):
        from_part(lax.rem(me + step, n_mp)).wait_recv()

    total = part_in[0].astype(jnp.float32)
    for source in range(1, n_mp):
        total = total + part_in[source].astype(jnp.float32)
    slot = lax.broadcasted_iota(jnp.int32, (seq, LANES), 0)
    for example in range(own):
        live = (slot < lengths[me * own + example]).astype(jnp.float32)
        rank_sum[me, example * seq:(example + 1) * seq, :] = (
            total[example * seq:(example + 1) * seq, :] * live
        ).astype(jnp.bfloat16)

    def send_rank(to):
        return pltpu.make_async_remote_copy(
            src_ref=rank_sum.at[me], dst_ref=rank_sum.at[me],
            send_sem=rank_send.at[to], recv_sem=rank_recv.at[me],
            device_id=(my_dp, to), device_id_type=MESH,
        )

    def from_rank(source):
        return pltpu.make_async_remote_copy(
            src_ref=rank_sum.at[source], dst_ref=rank_sum.at[source],
            send_sem=rank_send.at[source], recv_sem=rank_recv.at[source],
            device_id=(my_dp, source), device_id_type=MESH,
        )

    @pl.loop(1, n_mp)
    def _(step):
        send_rank(lax.rem(me + step, n_mp)).start()

    def send_raw(to):
        return pltpu.make_async_remote_copy(
            src_ref=raw.at[to], dst_ref=raw_in.at[me],
            send_sem=raw_send.at[to], recv_sem=raw_recv.at[me],
            device_id=(my_dp, to), device_id_type=MESH,
        )

    def from_raw(source):
        return pltpu.make_async_remote_copy(
            src_ref=raw.at[source], dst_ref=raw_in.at[source],
            send_sem=raw_send.at[source], recv_sem=raw_recv.at[source],
            device_id=(my_dp, source), device_id_type=MESH,
        )

    def raw_chunk(owner):
        left = lax.dot_general(
            rank_sum[owner], sign_rank[...], NT, preferred_element_type=jnp.float32
        )
        product = left * right[pl.ds(pl.multiple_of(owner * rows, rows), rows), :]
        sums = product.reshape(own, seq, product.shape[1]).sum(axis=1)
        return [
            sums[example:example + 1, block * LANES:(block + 1) * LANES]
            for example in range(own)
            for block in range(blocks)
        ]

    for at, line in enumerate(raw_chunk(me)):
        raw_in[me, at:at + 1, :] = line

    @pl.loop(1, n_mp)
    def _(step):
        owner = lax.rem(me + step, n_mp)
        from_rank(owner).wait_recv()
        for at, line in enumerate(raw_chunk(owner)):
            raw[owner, at:at + 1, :] = line
        send_raw(owner).start()

    @pl.loop(1, n_mp)
    def _(step):
        from_raw(lax.rem(me + step, n_mp)).wait_recv()

    raw_sum = raw_in[0]
    for source in range(1, n_mp):
        raw_sum = raw_sum + raw_in[source]
    for example in range(own):
        part_rows = raw_sum[example * blocks:(example + 1) * blocks, :]
        mean = jnp.sum(part_rows * part_rows, keepdims=True) / (blocks * LANES)
        mine[example * blocks:(example + 1) * blocks, :] = part_rows * lax.rsqrt(mean + 1e-06)
    group[me] = mine[...].astype(jnp.bfloat16)
    others[my_dp] = mine[...].astype(jnp.bfloat16)

    def send_group(to):
        return pltpu.make_async_remote_copy(
            src_ref=group.at[me], dst_ref=group.at[me],
            send_sem=group_send.at[to], recv_sem=group_recv.at[me],
            device_id=(my_dp, to), device_id_type=MESH,
        )

    def from_group(source):
        return pltpu.make_async_remote_copy(
            src_ref=group.at[source], dst_ref=group.at[source],
            send_sem=group_send.at[source], recv_sem=group_recv.at[source],
            device_id=(my_dp, source), device_id_type=MESH,
        )

    def send_other(to):
        return pltpu.make_async_remote_copy(
            src_ref=others.at[my_dp], dst_ref=others.at[my_dp],
            send_sem=other_send.at[to], recv_sem=other_recv.at[my_dp],
            device_id=(to, me), device_id_type=MESH,
        )

    def from_other(source):
        return pltpu.make_async_remote_copy(
            src_ref=others.at[source], dst_ref=others.at[source],
            send_sem=other_send.at[source], recv_sem=other_recv.at[source],
            device_id=(source, me), device_id_type=MESH,
        )

    @pl.loop(1, n_dp)
    def _(step):
        send_other(lax.rem(my_dp + step, n_dp)).start()

    @pl.loop(1, n_mp)
    def _(step):
        send_group(lax.rem(me + step, n_mp)).start()

    sketch_out[...] = jnp.concatenate(
        [mine[pl.ds(block, own, stride=blocks), :] for block in range(blocks)], axis=1
    ).astype(jnp.bfloat16)

    @pl.loop(1, n_mp)
    def _(step):
        to = lax.rem(me + step, n_mp)
        send_part(to).wait_send()
        send_rank(to).wait_send()
        send_raw(to).wait_send()

    @pl.loop(1, n_mp)
    def _(step):
        from_group(lax.rem(me + step, n_mp)).wait_recv()

    group_f[...] = group[...].astype(jnp.float32).reshape(n_mp * width, LANES)

    @pl.loop(1, n_dp)
    def _(step):
        from_other(lax.rem(my_dp + step, n_dp)).wait_recv()

    others_f[...] = others[...].astype(jnp.float32).reshape(n_dp * width, LANES)

    for example in range(own):
        cosines = jnp.zeros((n_mp * own, n_dp), jnp.float32)
        for block in range(blocks):
            here = group_f[pl.ds(block, n_mp * own, stride=blocks), :].astype(jnp.bfloat16)
            there = others_f[pl.ds(example * blocks + block, n_dp, stride=width), :]
            cosines = cosines + lax.dot_general(
                here, there.astype(jnp.bfloat16), NT, preferred_element_type=jnp.float32
            )
        cos_out[example] = cosines / (blocks * LANES)

    @pl.loop(1, n_mp)
    def _(step):
        send_group(lax.rem(me + step, n_mp)).wait_send()

    @pl.loop(1, n_dp)
    def _(step):
        send_other(lax.rem(my_dp + step, n_dp)).wait_send()


def solution(mesh):
    n_dp, n_mp = mesh.shape["dp"], mesh.shape["mp"]

    def per_device(activations, gradients, up_matrix, rank_words, feat_words, lengths):
        examples = lengths.shape[0]
        tokens, features = activations.shape
        seq = tokens // examples
        own = examples // n_mp
        rank = up_matrix.shape[1]
        sketch = 16 * rank_words.shape[0]
        width = own * sketch // LANES
        rows = own * seq
        bf16, f32, dma = jnp.bfloat16, jnp.float32, pltpu.SemaphoreType.DMA
        anywhere = pl.BlockSpec(memory_space=pl.ANY)
        sketches, cosines = pl.pallas_call(
            functools.partial(kernel, n_dp, n_mp, seq),
            out_shape=[
                jax.ShapeDtypeStruct((own, sketch), bf16),
                jax.ShapeDtypeStruct((own, examples, n_dp), f32),
            ],
            in_specs=[anywhere] * 5 + [pl.BlockSpec(memory_space=pltpu.SMEM)],
            out_specs=[pl.BlockSpec(memory_space=pltpu.VMEM)] * 2,
            scratch_shapes=[
                pltpu.VMEM((tokens, features), bf16),
                pltpu.VMEM((tokens, features), bf16),
                pltpu.VMEM((features, rank), bf16),
                pltpu.VMEM(rank_words.shape, jnp.int32),
                pltpu.VMEM(feat_words.shape, jnp.int32),
                dma((5,)),
                pltpu.VMEM((sketch, rank), bf16),
                pltpu.VMEM((sketch, features), bf16),
                pltpu.VMEM((tokens, sketch), f32),
                pltpu.VMEM((n_mp, rows, rank), bf16),
                pltpu.VMEM((n_mp, rows, rank), bf16),
                pltpu.VMEM((n_mp, rows, rank), bf16),
                pltpu.VMEM((n_mp, width, LANES), f32),
                pltpu.VMEM((n_mp, width, LANES), f32),
                pltpu.VMEM((width, LANES), f32),
                pltpu.VMEM((n_mp, width, LANES), bf16),
                pltpu.VMEM((n_dp, width, LANES), bf16),
                pltpu.VMEM((n_mp * width, LANES), f32),
                pltpu.VMEM((n_dp * width, LANES), f32),
            ]
            + [dma((n_mp,))] * 8
            + [dma((n_dp,))] * 2,
            compiler_params=pltpu.CompilerParams(
                collective_id=0, has_side_effects=True, vmem_limit_bytes=32 * 1024 * 1024
            ),
        )(activations, gradients, up_matrix, rank_words, feat_words, lengths)
        return sketches, cosines.transpose(1, 2, 0)

    return jax.shard_map(
        per_device,
        mesh=mesh,
        in_specs=(P("dp", "mp"), P("dp", "mp"), P("mp", None), P(), P(None, "mp"), P("dp")),
        out_specs=(P(("dp", "mp"), None), P("dp", None, "mp")),
        check_vma=False,
    )
```

```python
import functools

import jax
import jax.numpy as jnp
from jax import lax
from jax.experimental import pallas as pl
from jax.experimental.pallas import tpu as pltpu
from jax.sharding import PartitionSpec as P

MESH = pl.DeviceIdType.MESH
NT = (((1,), (1,)), ((), ()))
LANES = 128
NX, NZ = 4, 4
NY, NC = 8, 4


def far_first(step, count):
    return count // 2 + (1 - 2 * (step % 2)) * ((step + 1) // 2)


def unpack_signs(words):
    shape = (words.shape[0], 16, words.shape[1])
    offsets = lax.broadcasted_iota(jnp.int32, shape, 1)
    bits = jnp.bitwise_and(jnp.right_shift(words[:, None, :], offsets), 1)
    signs = (2 * bits - 1).astype(jnp.float32).astype(jnp.bfloat16)
    return signs.reshape(shape[0] * 16, shape[2])


def kernel(
    n_dp, n_mp, seq,
    act_hbm, grad_hbm, up_hbm, rank_words_hbm, feat_words_hbm, lengths_hbm,
    sketch_out, cos_out,
    grad, up, rank_words, lengths, up_sem, grad_sem, rank_words_sem, lengths_sem,
    act_in, words_in, part, part_in, zsum, sign_rank, sign_feat, right, rank_pair,
    raw, raw_in, mine, group, others, group_f, others_f,
    act_send, act_recv, words_send, words_recv, part_send, part_recv, zsum_send, zsum_recv,
    raw_send, raw_recv, group_send, group_recv, other_send, other_recv,
):
    my_dp = lax.axis_index("dp")
    me = lax.axis_index("mp")
    x, z = me // NZ, me % NZ
    quarter = part.shape[1]
    examples = quarter // seq
    own = examples // NZ
    rows = own * seq
    sketch = sign_feat.shape[0]
    blocks = sketch // LANES
    width = own * blocks
    steps_x = [far_first(step, NX) for step in range(NX - 1)]
    steps_z = [far_first(step, NZ) for step in range(NZ - 1)]

    def rows_of(ref, at):
        return ref.at[pl.ds(pl.multiple_of(at * quarter, quarter), quarter), :]

    def remote(src, dst, send_sem, recv_sem, to_dp, to_mp):
        return pltpu.make_async_remote_copy(
            src_ref=src, dst_ref=dst, send_sem=send_sem, recv_sem=recv_sem,
            device_id=(to_dp, to_mp), device_id_type=MESH,
        )

    load_up = pltpu.make_async_copy(up_hbm, up, up_sem)
    load_grad = pltpu.make_async_copy(grad_hbm, grad, grad_sem)
    load_words = pltpu.make_async_copy(feat_words_hbm, words_in.at[x], words_recv.at[x])
    load_act = pltpu.make_async_copy(rows_of(act_hbm, x), act_in.at[x], act_recv.at[x])
    load_rank_words = pltpu.make_async_copy(rank_words_hbm, rank_words, rank_words_sem)
    load_lengths = pltpu.make_async_copy(lengths_hbm, lengths, lengths_sem)
    for load in (load_up, load_grad, load_words, load_act, load_rank_words, load_lengths):
        load.start()

    barrier = pltpu.get_barrier_semaphore()

    def mp_peer(step):
        return (x + far_first(step % NX, NX)) % NX * NZ + (z + far_first(step // NX, NZ)) % NZ

    def dp_peer(step):
        return (my_dp // NC + far_first(step // NC, NY)) % NY * NC + (
            my_dp % NC + (NC - 1 - step % NC)
        ) % NC

    @pl.loop(0, n_dp - 1)
    def _(step):
        pl.semaphore_signal(barrier, inc=1, device_id=(dp_peer(step), me), device_id_type=MESH)

    @pl.loop(0, n_mp - 1)
    def _(step):
        pl.semaphore_signal(barrier, inc=1, device_id=(my_dp, mp_peer(step)), device_id_type=MESH)

    load_up.wait()
    load_grad.wait()
    for step in range(NX):
        to = (x + far_first(step, NX)) % NX
        tokens = grad[pl.ds(pl.multiple_of(to * quarter, quarter), quarter), :]
        part[to] = jnp.dot(tokens, up[...], preferred_element_type=jnp.float32).astype(jnp.bfloat16)
    pl.semaphore_wait(barrier, n_mp + n_dp - 2)

    def send_part(to):
        return remote(
            part.at[to], part_in.at[x], part_send.at[to], part_recv.at[x], my_dp, to * NZ + z
        )

    def send_words(to):
        return remote(
            feat_words_hbm, words_in.at[x], words_send.at[to], words_recv.at[x], my_dp, to * NZ + z
        )

    def send_act(to):
        return remote(
            rows_of(act_hbm, to), act_in.at[x], act_send.at[to], act_recv.at[x], my_dp, to * NZ + z
        )

    for step in steps_x:
        send_part((x + step) % NX).start()
    for step in steps_x:
        send_words((x + step) % NX).start()
    for step in steps_x:
        send_act((x + step) % NX).start()

    load_rank_words.wait()
    signs = unpack_signs(rank_words[...])
    sign_rank[...] = jnp.concatenate([signs, signs], axis=1)

    def arrived(ref, sems, source):
        return remote(ref.at[source], ref.at[source], sems.at[source], sems.at[source], my_dp, me)

    load_words.wait()
    sign_feat[...] = unpack_signs(words_in[x])
    load_act.wait()
    right[...] = lax.dot_general(
        act_in[x], sign_feat[...], NT, preferred_element_type=jnp.float32
    )

    for step in steps_x:
        arrived(part_in, part_recv, (x + step) % NX).wait_recv()
    total = part[x].astype(jnp.float32)
    for step in steps_x:
        total = total + part_in[(x + step) % NX].astype(jnp.float32)
    zsum[z] = total.astype(jnp.bfloat16)

    def send_zsum(to):
        return remote(
            zsum.at[z], zsum.at[z], zsum_send.at[to], zsum_recv.at[z], my_dp, x * NZ + to
        )

    for step in steps_z:
        send_zsum((z + step) % NZ).start()

    for step in (1, 3, 2):
        source = (x + step) % NX
        arrived(words_in, words_recv, source).wait_recv()
        sign_feat[...] = unpack_signs(words_in[source])
        arrived(act_in, act_recv, source).wait_recv()
        right[...] += lax.dot_general(
            act_in[source], sign_feat[...], NT, preferred_element_type=jnp.float32
        )

    load_lengths.wait()
    for step in steps_z:
        arrived(zsum, zsum_recv, (z + step) % NZ).wait_recv()
    slot = lax.broadcasted_iota(jnp.int32, (seq, LANES), 0)
    for example in range(examples):
        at = slice(example * seq, (example + 1) * seq)
        total = zsum[0, at, :].astype(jnp.float32)
        for source in range(1, NZ):
            total = total + zsum[source, at, :].astype(jnp.float32)
        total = total * (slot < lengths[x * examples + example]).astype(jnp.float32)
        high = total.astype(jnp.bfloat16)
        rank_pair[at, :LANES] = high
        rank_pair[at, LANES:] = (total - high.astype(jnp.float32)).astype(jnp.bfloat16)

    def send_raw(to):
        return remote(
            raw.at[to], raw_in.at[z], raw_send.at[to], raw_recv.at[z], my_dp, x * NZ + to
        )

    for step in steps_z + [0]:
        owner = (z + step) % NZ
        at = pl.ds(pl.multiple_of(owner * rows, rows), rows)
        left = lax.dot_general(
            rank_pair[at, :], sign_rank[...], NT, preferred_element_type=jnp.float32
        )
        sums = (left * right[at, :]).reshape(own, seq, sketch).sum(axis=1)
        for example in range(own):
            for block in range(blocks):
                line = example * blocks + block
                raw[owner, line:line + 1, :] = sums[
                    example:example + 1, block * LANES:(block + 1) * LANES
                ]
        if step:
            send_raw(owner).start()

    raw_sum = raw[z]
    for step in steps_z:
        source = (z + step) % NZ
        arrived(raw_in, raw_recv, source).wait_recv()
        raw_sum = raw_sum + raw_in[source]
    for example in range(own):
        lines = raw_sum[example * blocks:(example + 1) * blocks, :]
        mean = jnp.sum(lines * lines, keepdims=True) / sketch
        mine[example * blocks:(example + 1) * blocks, :] = lines * lax.rsqrt(mean + 1e-06)
    group[me] = mine[...].astype(jnp.bfloat16)
    others[my_dp] = mine[...].astype(jnp.bfloat16)

    def send_group(to):
        return remote(
            group.at[me], group.at[me], group_send.at[to], group_recv.at[me], my_dp, to
        )

    def send_other(to):
        return remote(
            others.at[my_dp], others.at[my_dp], other_send.at[to], other_recv.at[my_dp], to, me
        )

    @pl.loop(0, n_dp - 1)
    def _(step):
        send_other(dp_peer(step)).start()

        @pl.when(step < n_mp - 1)
        def _():
            send_group(mp_peer(step)).start()

    sketch_out[...] = jnp.concatenate(
        [mine[pl.ds(block, own, stride=blocks), :] for block in range(blocks)], axis=1
    ).astype(jnp.bfloat16)

    for step in steps_x:
        to = (x + step) % NX
        send_part(to).wait_send()
        send_words(to).wait_send()
        send_act(to).wait_send()
    for step in steps_z:
        to = (z + step) % NZ
        send_zsum(to).wait_send()
        send_raw(to).wait_send()

    @pl.loop(0, n_mp - 1)
    def _(step):
        arrived(group, group_recv, mp_peer(step)).wait_recv()

    group_f[...] = group[...].astype(jnp.float32).reshape(n_mp * width, LANES)

    @pl.loop(0, n_dp - 1)
    def _(step):
        arrived(others, other_recv, dp_peer(step)).wait_recv()

    others_f[...] = others[...].astype(jnp.float32).reshape(n_dp * width, LANES)

    for example in range(own):
        cosines = jnp.zeros((n_mp * own, n_dp), jnp.float32)
        for block in range(blocks):
            here = group_f[pl.ds(block, n_mp * own, stride=blocks), :].astype(jnp.bfloat16)
            there = others_f[pl.ds(example * blocks + block, n_dp, stride=width), :]
            cosines = cosines + lax.dot_general(
                here, there.astype(jnp.bfloat16), NT, preferred_element_type=jnp.float32
            )
        cos_out[example] = cosines / sketch

    @pl.loop(0, n_mp - 1)
    def _(step):
        send_group(mp_peer(step)).wait_send()

    @pl.loop(0, n_dp - 1)
    def _(step):
        send_other(dp_peer(step)).wait_send()


def solution(mesh):
    n_dp, n_mp = mesh.shape["dp"], mesh.shape["mp"]

    def per_device(activations, gradients, up_matrix, rank_words, feat_words, lengths):
        examples = lengths.shape[0]
        tokens, features = activations.shape
        seq = tokens // examples
        own = examples // n_mp
        rank = up_matrix.shape[1]
        sketch = 16 * rank_words.shape[0]
        width = own * sketch // LANES
        quarter = tokens // NX
        bf16, f32, dma = jnp.bfloat16, jnp.float32, pltpu.SemaphoreType.DMA
        in_hbm = pl.BlockSpec(memory_space=pltpu.HBM)
        sketches, cosines = pl.pallas_call(
            functools.partial(kernel, n_dp, n_mp, seq),
            out_shape=[
                jax.ShapeDtypeStruct((own, sketch), bf16),
                jax.ShapeDtypeStruct((own, examples, n_dp), f32),
            ],
            in_specs=[in_hbm] * 6,
            out_specs=[pl.BlockSpec(memory_space=pltpu.VMEM)] * 2,
            scratch_shapes=[
                pltpu.VMEM((tokens, features), bf16),
                pltpu.VMEM((features, rank), bf16),
                pltpu.VMEM(rank_words.shape, jnp.int32),
                pltpu.SMEM((examples,), jnp.int32),
                dma(()),
                dma(()),
                dma(()),
                dma(()),
                pltpu.VMEM((NX, quarter, features), bf16),
                pltpu.VMEM((NX,) + feat_words.shape, jnp.int32),
                pltpu.VMEM((NX, quarter, rank), bf16),
                pltpu.VMEM((NX, quarter, rank), bf16),
                pltpu.VMEM((NZ, quarter, rank), bf16),
                pltpu.VMEM((sketch, 2 * rank), bf16),
                pltpu.VMEM((sketch, features), bf16),
                pltpu.VMEM((quarter, sketch), f32),
                pltpu.VMEM((quarter, 2 * rank), bf16),
                pltpu.VMEM((NZ, width, LANES), f32),
                pltpu.VMEM((NZ, width, LANES), f32),
                pltpu.VMEM((width, LANES), f32),
                pltpu.VMEM((n_mp, width, LANES), bf16),
                pltpu.VMEM((n_dp, width, LANES), bf16),
                pltpu.VMEM((n_mp * width, LANES), f32),
                pltpu.VMEM((n_dp * width, LANES), f32),
            ]
            + [dma((NX,))] * 6
            + [dma((NZ,))] * 4
            + [dma((n_mp,))] * 2
            + [dma((n_dp,))] * 2,
            compiler_params=pltpu.CompilerParams(
                collective_id=0, has_side_effects=True, vmem_limit_bytes=64 * 1024 * 1024
            ),
        )(activations, gradients, up_matrix, rank_words, feat_words, lengths)
        return sketches, cosines.transpose(1, 2, 0)

    return jax.shard_map(
        per_device,
        mesh=mesh,
        in_specs=(P("dp", "mp"), P("dp", "mp"), P("mp", None), P(), P(None, "mp"), P("dp")),
        out_specs=(P(("dp", "mp"), None), P("dp", None, "mp")),
        check_vma=False,
    )
```

```python
import functools

import jax
import jax.numpy as jnp
from jax import lax
from jax.experimental import pallas as pl
from jax.experimental.pallas import tpu as pltpu
from jax.sharding import PartitionSpec as P

MESH = pl.DeviceIdType.MESH
NT = (((1,), (1,)), ((), ()))
LANES = 128
NX, NZ = 4, 4
NY, NC = 8, 4


def far_first(count):
    return sorted(range(1, count), key=lambda step: -min(step, count - step))


def unpack_signs(words):
    words = words.astype(jnp.int32)
    shape = (words.shape[0], 16, words.shape[1])
    offsets = lax.broadcasted_iota(jnp.int32, shape, 1)
    bits = jnp.bitwise_and(jnp.right_shift(words[:, None, :], offsets), 1)
    signs = (2 * bits - 1).astype(jnp.float32).astype(jnp.bfloat16)
    return signs.reshape(shape[0] * 16, shape[2])


def kernel(
    n_dp, n_mp, seq,
    act_hbm, grad_hbm, up_hbm, rank_words_hbm, feat_words_hbm, lengths_hbm,
    sketch_out, cos_out,
    grad, up, rank_words, feat_words, lengths,
    up_sem, grad_sem, rank_words_sem, feat_words_sem, lengths_sem,
    act_in, words_in, part, part_in, zsum, sign_rank, sign_feat, right,
    raw, raw_in, mine, group, others, group_f, others_f,
    act_send, act_recv, words_send, words_recv, part_send, part_recv, zsum_send, zsum_recv,
    raw_send, raw_recv, group_send, group_recv, other_send, other_recv,
):
    my_dp = lax.axis_index("dp")
    me = lax.axis_index("mp")
    x, z = me // NZ, me % NZ
    y, core = my_dp // NC, my_dp % NC
    rows = part.shape[2]
    quarter = NZ * rows
    own = rows // seq
    examples = NZ * own
    sketch = sign_feat.shape[0]
    blocks = sketch // LANES
    width = own * blocks
    ring_x = [(x + step) % NX for step in far_first(NX)]
    ring_z = [(z + step) % NZ for step in far_first(NZ)]
    ring_y = [(y + step) % NY for step in far_first(NY)]
    ring_c = [(core + step) % NC for step in range(1, NC)]
    mp_peers = [to_x * NZ + to_z for to_z in ring_z for to_x in ring_x + [x]]
    mp_peers += [to_x * NZ + z for to_x in ring_x]
    dp_peers = [to_y * NC + to_c for to_y in ring_y for to_c in ring_c + [core]]
    dp_peers += [y * NC + to_c for to_c in ring_c]

    def rows_of(ref, at):
        return ref.at[pl.ds(pl.multiple_of(at * quarter, quarter), quarter), :]

    def remote(src, dst, send_sem, recv_sem, to_dp, to_mp):
        return pltpu.make_async_remote_copy(
            src_ref=src, dst_ref=dst, send_sem=send_sem, recv_sem=recv_sem,
            device_id=(to_dp, to_mp), device_id_type=MESH,
        )

    def arrived(ref, sem):
        return remote(ref, ref, sem, sem, my_dp, me)

    load_up = pltpu.make_async_copy(up_hbm, up, up_sem)
    load_grad = pltpu.make_async_copy(grad_hbm, grad, grad_sem)
    load_words = pltpu.make_async_copy(feat_words_hbm, feat_words, feat_words_sem)
    load_act = pltpu.make_async_copy(rows_of(act_hbm, x), act_in.at[x], act_recv.at[x])
    load_rank_words = pltpu.make_async_copy(rank_words_hbm, rank_words, rank_words_sem)
    load_lengths = pltpu.make_async_copy(lengths_hbm, lengths, lengths_sem)
    for load in (load_up, load_grad, load_words, load_act, load_rank_words, load_lengths):
        load.start()

    barrier = pltpu.get_barrier_semaphore()
    for to in mp_peers:
        pl.semaphore_signal(barrier, inc=1, device_id=(my_dp, to), device_id_type=MESH)
    for to in dp_peers:
        pl.semaphore_signal(barrier, inc=1, device_id=(to, me), device_id_type=MESH)

    load_up.wait()
    load_grad.wait()
    for to in ring_x + [x]:
        tokens = grad[pl.ds(pl.multiple_of(to * quarter, quarter), quarter), :]
        part[to] = (
            jnp.dot(tokens, up[...], preferred_element_type=jnp.float32)
            .astype(jnp.bfloat16)
            .reshape(NZ, rows, LANES)
        )
    load_words.wait()
    words_in[x] = feat_words[...].astype(jnp.int16)
    pl.semaphore_wait(barrier, n_mp + n_dp - 2)

    def send_part(to, piece):
        return remote(
            part.at[to, piece], part_in.at[x, piece],
            part_send.at[to, piece], part_recv.at[x, piece], my_dp, to * NZ + z,
        )

    def send_words(to):
        return remote(
            words_in.at[x], words_in.at[x], words_send.at[to], words_recv.at[x], my_dp, to * NZ + z
        )

    def send_act(to):
        return remote(
            rows_of(act_hbm, to), act_in.at[x], act_send.at[to], act_recv.at[x], my_dp, to * NZ + z
        )

    for piece in range(NZ):
        for to in ring_x:
            send_part(to, piece).start()
    for to in ring_x:
        send_words(to).start()
    for to in ring_x:
        send_act(to).start()

    load_rank_words.wait()
    signs = unpack_signs(rank_words[...])
    sign_rank[...] = jnp.concatenate([signs, signs], axis=1)
    sign_feat[...] = unpack_signs(words_in[x])
    load_act.wait()
    right[...] = lax.dot_general(
        act_in[x], sign_feat[...], NT, preferred_element_type=jnp.float32
    )

    def send_zsum(to, piece):
        return remote(
            zsum.at[z, piece], zsum.at[z, piece],
            zsum_send.at[to, piece], zsum_recv.at[z, piece], my_dp, x * NZ + to,
        )

    for piece in range(NZ):
        total = part[x, piece].astype(jnp.float32)
        for source in ring_x:
            arrived(part_in.at[source, piece], part_recv.at[source, piece]).wait_recv()
            total = total + part_in[source, piece].astype(jnp.float32)
        zsum[z, piece] = total.astype(jnp.bfloat16)
        for to in ring_z:
            send_zsum(to, piece).start()

    for source in ring_x[1:] + ring_x[:1]:
        arrived(words_in.at[source], words_recv.at[source]).wait_recv()
        sign_feat[...] = unpack_signs(words_in[source])
        arrived(act_in.at[source], act_recv.at[source]).wait_recv()
        right[...] += lax.dot_general(
            act_in[source], sign_feat[...], NT, preferred_element_type=jnp.float32
        )

    load_lengths.wait()
    slot = lax.broadcasted_iota(jnp.int32, (seq, LANES), 0)

    def send_raw(to):
        return remote(
            raw.at[to], raw_in.at[z], raw_send.at[to], raw_recv.at[z], my_dp, x * NZ + to
        )

    for piece in range(NZ):
        total = zsum[z, piece].astype(jnp.float32)
        for source in ring_z:
            arrived(zsum.at[source, piece], zsum_recv.at[source, piece]).wait_recv()
            total = total + zsum[source, piece].astype(jnp.float32)
        live = jnp.concatenate(
            [
                (slot < lengths[x * examples + piece * own + example]).astype(jnp.float32)
                for example in range(own)
            ]
        )
        total = total * live
        high = total.astype(jnp.bfloat16)
        low = (total - high.astype(jnp.float32)).astype(jnp.bfloat16)
        left = lax.dot_general(
            jnp.concatenate([high, low], axis=1), sign_rank[...], NT,
            preferred_element_type=jnp.float32,
        )
        product = left * right[piece * rows:(piece + 1) * rows, :]
        sums = product.reshape(own, seq, sketch).sum(axis=1)
        for example in range(own):
            for block in range(blocks):
                line = example * blocks + block
                raw[piece, line:line + 1, :] = sums[
                    example:example + 1, block * LANES:(block + 1) * LANES
                ]

        @pl.when(z != piece)
        def _():
            send_raw(piece).start()

    raw_sum = raw[z]
    for source in ring_z:
        arrived(raw_in.at[source], raw_recv.at[source]).wait_recv()
        raw_sum = raw_sum + raw_in[source]
    for example in range(own):
        lines = raw_sum[example * blocks:(example + 1) * blocks, :]
        mean = jnp.sum(lines * lines, keepdims=True) / sketch
        mine[example * blocks:(example + 1) * blocks, :] = lines * lax.rsqrt(mean + 1e-06)
    group[me] = mine[...].astype(jnp.bfloat16)
    others[my_dp] = mine[...].astype(jnp.bfloat16)

    for at, to in enumerate(dp_peers):
        remote(
            others.at[my_dp], others.at[my_dp], other_send, other_recv, to, me
        ).start()
        if at < len(mp_peers):
            remote(
                group.at[me], group.at[me], group_send, group_recv, my_dp, mp_peers[at]
            ).start()

    sketch_out[...] = jnp.concatenate(
        [mine[pl.ds(block, own, stride=blocks), :] for block in range(blocks)], axis=1
    ).astype(jnp.bfloat16)

    for to in ring_x:
        for piece in range(NZ):
            send_part(to, piece).wait_send()
        send_words(to).wait_send()
        send_act(to).wait_send()
    for to in ring_z:
        for piece in range(NZ):
            send_zsum(to, piece).wait_send()
        send_raw(to).wait_send()
    remote(
        group.at[pl.ds(0, n_mp - 1)], group.at[pl.ds(0, n_mp - 1)], group_send, group_recv, my_dp, me
    ).wait()
    group_f[...] = group[...].astype(jnp.float32).reshape(n_mp * width, LANES)
    remote(
        others.at[pl.ds(0, n_dp - 1)], others.at[pl.ds(0, n_dp - 1)], other_send, other_recv, my_dp, me
    ).wait()
    others_f[...] = others[...].astype(jnp.float32).reshape(n_dp * width, LANES)

    for example in range(own):
        cosines = jnp.zeros((n_mp * own, n_dp), jnp.float32)
        for block in range(blocks):
            here = group_f[pl.ds(block, n_mp * own, stride=blocks), :].astype(jnp.bfloat16)
            there = others_f[pl.ds(example * blocks + block, n_dp, stride=width), :]
            cosines = cosines + lax.dot_general(
                here, there.astype(jnp.bfloat16), NT, preferred_element_type=jnp.float32
            )
        cos_out[:, example, :] = cosines / sketch


def solution(mesh):
    n_dp, n_mp = mesh.shape["dp"], mesh.shape["mp"]

    def per_device(activations, gradients, up_matrix, rank_words, feat_words, lengths):
        examples = lengths.shape[0]
        tokens, features = activations.shape
        seq = tokens // examples
        own = examples // n_mp
        rank = up_matrix.shape[1]
        sketch = 16 * rank_words.shape[0]
        width = own * sketch // LANES
        quarter = tokens // NX
        pieces = (NX, NZ, own * seq, rank)
        bf16, f32, dma = jnp.bfloat16, jnp.float32, pltpu.SemaphoreType.DMA
        in_hbm = pl.BlockSpec(memory_space=pltpu.HBM)
        sketches, cosines = pl.pallas_call(
            functools.partial(kernel, n_dp, n_mp, seq),
            out_shape=[
                pltpu.VMEM((own, sketch), bf16),
                pltpu.VMEM((examples, own, n_dp), f32),
            ],
            in_specs=[in_hbm] * 6,
            out_specs=[pl.BlockSpec(memory_space=pltpu.VMEM)] * 2,
            scratch_shapes=[
                pltpu.VMEM((tokens, features), bf16),
                pltpu.VMEM((features, rank), bf16),
                pltpu.VMEM(rank_words.shape, jnp.int32),
                pltpu.VMEM(feat_words.shape, jnp.int32),
                pltpu.SMEM((examples,), jnp.int32),
                dma(()),
                dma(()),
                dma(()),
                dma(()),
                dma(()),
                pltpu.VMEM((NX, quarter, features), bf16),
                pltpu.VMEM((NX,) + feat_words.shape, jnp.int16),
                pltpu.VMEM(pieces, bf16),
                pltpu.VMEM(pieces, bf16),
                pltpu.VMEM((NZ,) + pieces[1:], bf16),
                pltpu.VMEM((sketch, 2 * rank), bf16),
                pltpu.VMEM((sketch, features), bf16),
                pltpu.VMEM((quarter, sketch), f32),
                pltpu.VMEM((NZ, width, LANES), f32),
                pltpu.VMEM((NZ, width, LANES), f32),
                pltpu.VMEM((width, LANES), f32),
                pltpu.VMEM((n_mp, width, LANES), bf16),
                pltpu.VMEM((n_dp, width, LANES), bf16),
                pltpu.VMEM((n_mp * width, LANES), f32),
                pltpu.VMEM((n_dp * width, LANES), f32),
            ]
            + [dma((NX,))] * 4
            + [dma((NX, NZ))] * 2
            + [dma((NZ, NZ))] * 2
            + [dma((NZ,))] * 2
            + [dma(())] * 4,
            compiler_params=pltpu.CompilerParams(
                collective_id=0, has_side_effects=True, vmem_limit_bytes=48 * 1024 * 1024
            ),
        )(*[pltpu.with_memory_space_constraint(each, pltpu.HBM) for each in (activations, gradients, up_matrix, rank_words, feat_words, lengths)])
        return sketches, cosines.transpose(0, 2, 1)

    return jax.shard_map(
        per_device,
        mesh=mesh,
        in_specs=(P("dp", "mp"), P("dp", "mp"), P("mp", None), P(), P(None, "mp"), P("dp")),
        out_specs=(P(("dp", "mp"), None), P("dp", None, "mp")),
        check_vma=False,
    )
```

```python
import functools

import jax
import jax.numpy as jnp
from jax import lax
from jax.experimental import pallas as pl
from jax.experimental.pallas import tpu as pltpu
from jax.sharding import PartitionSpec as P

MESH = pl.DeviceIdType.MESH
NT = (((1,), (1,)), ((), ()))
LANES = 128
NX, NZ = 4, 4
NY, NC = 8, 4


def far_first(count):
    return sorted(range(1, count), key=lambda step: -min(step, count - step))


def unpack_signs(words):
    words = words.astype(jnp.int32)
    shape = (words.shape[0], 16, words.shape[1])
    offsets = lax.broadcasted_iota(jnp.int32, shape, 1)
    bits = jnp.bitwise_and(jnp.right_shift(words[:, None, :], offsets), 1)
    signs = (2 * bits - 1).astype(jnp.float32).astype(jnp.bfloat16)
    return signs.reshape(shape[0] * 16, shape[2])


def kernel(
    n_dp, n_mp, seq,
    act_hbm, grad_hbm, up_hbm, rank_words_hbm, feat_words_hbm, lengths_hbm,
    sketch_out, cos_out,
    grad, up, rank_words, feat_words, lengths,
    up_sem, grad_sem, rank_words_sem, feat_words_sem, lengths_sem,
    act_in, words_in, part, part_in, rank_sum, near_out, near_in, far_out, far_in,
    sign_rank, sign_feat, right,
    raw, raw_in, mine, group, others, group_f, others_f,
    act_send, act_recv, words_send, words_recv, twin_send, twin_recv, part_send, part_recv,
    near_send, near_recv, far_send, far_recv, raw_send, raw_recv,
    group_send, group_recv, other_send, other_recv, word_y, word_z,
):
    my_dp = lax.axis_index("dp")
    me = lax.axis_index("mp")
    x, z = me // NZ, me % NZ
    y, core = my_dp // NC, my_dp % NC
    rows = part.shape[2]
    quarter = NZ * rows
    own = rows // seq
    examples = NZ * own
    sketch = sign_feat.shape[0]
    blocks = sketch // LANES
    width = own * blocks
    ring_x = [(x + step) % NX for step in far_first(NX)]
    ring_z = [(z + step) % NZ for step in far_first(NZ)]
    ring_y = [(y + step) % NY for step in far_first(NY)]
    ring_c = [(core + step) % NC for step in range(1, NC)]
    mp_peers = [to_x * NZ + to_z for to_z in ring_z for to_x in ring_x + [x]]
    mp_peers += [to_x * NZ + z for to_x in ring_x]
    dp_peers = [to_y * NC + to_c for to_y in ring_y for to_c in ring_c + [core]]
    dp_peers += [y * NC + to_c for to_c in ring_c]

    def rows_of(ref, at):
        return ref.at[pl.ds(pl.multiple_of(at * quarter, quarter), quarter), :]

    def remote(src, dst, send_sem, recv_sem, to_dp, to_mp):
        return pltpu.make_async_remote_copy(
            src_ref=src, dst_ref=dst, send_sem=send_sem, recv_sem=recv_sem,
            device_id=(to_dp, to_mp), device_id_type=MESH,
        )

    def arrived(ref, sem):
        return remote(ref, ref, sem, sem, my_dp, me)

    half = my_dp % 2
    twin = my_dp + 1 - 2 * half
    near = z + 1 - 2 * (z % 2)
    far = NZ - 1 - z
    greeted = [(my_dp, to_x * NZ + z) for to_x in ring_x]
    greeted += [(my_dp, x * NZ + near), (my_dp, x * NZ + far), (twin, me)]
    barrier = pltpu.get_barrier_semaphore()
    for to in greeted:
        pl.semaphore_signal(barrier, inc=1, device_id=to, device_id_type=MESH)

    load_up = pltpu.make_async_copy(up_hbm, up, up_sem)
    load_grad = pltpu.make_async_copy(grad_hbm, grad, grad_sem)
    load_words = pltpu.make_async_copy(feat_words_hbm, feat_words, feat_words_sem)
    load_act = pltpu.make_async_copy(rows_of(act_hbm, x), act_in.at[x], act_recv.at[x])
    load_rank_words = pltpu.make_async_copy(rank_words_hbm, rank_words, rank_words_sem)
    load_lengths = pltpu.make_async_copy(lengths_hbm, lengths, lengths_sem)
    for load in (load_up, load_grad, load_words, load_act, load_rank_words, load_lengths):
        load.start()

    @pl.when(z == 0)
    def _():
        for to in dp_peers:
            pl.semaphore_signal(barrier, inc=1, device_id=(to, me), device_id_type=MESH)

    load_up.wait()
    load_grad.wait()
    for to in ring_x + [x]:
        tokens = grad[pl.ds(pl.multiple_of(to * quarter, quarter), quarter), :]
        part[to] = (
            jnp.dot(tokens, up[...], preferred_element_type=jnp.float32)
            .astype(jnp.bfloat16)
            .reshape(NZ, rows, LANES)
        )
    load_words.wait()
    half_words = feat_words.shape[0] // 2
    for at in range(2):
        words_in[at, x] = feat_words[at * half_words:(at + 1) * half_words, :].astype(jnp.int16)

    @pl.when(z == 0)
    def _():
        pl.semaphore_wait(barrier, len(greeted) + len(dp_peers))

    @pl.when(z != 0)
    def _():
        pl.semaphore_wait(barrier, len(greeted))

    def send_part(to, piece):
        return remote(
            part.at[to, piece], part_in.at[x, piece],
            part_send.at[to, piece], part_recv.at[x, piece], my_dp, to * NZ + z,
        )

    def send_words(to):
        return remote(
            words_in.at[half, x], words_in.at[half, x],
            words_send.at[to], words_recv.at[x], my_dp, to * NZ + z,
        )

    def send_twin(source):
        return remote(
            words_in.at[half, source], words_in.at[half, source],
            twin_send.at[source], twin_recv.at[source], twin, me,
        )

    def send_act(to):
        return remote(
            rows_of(act_hbm, to), act_in.at[x], act_send.at[to], act_recv.at[x], my_dp, to * NZ + z
        )

    for piece in range(NZ):
        for to in ring_x:
            send_part(to, piece).start()
    for to in ring_x:
        send_words(to).start()
    for to in ring_x:
        send_act(to).start()

    def unpack_slice(source):
        for at in range(2):
            sign_feat[at * sketch // 2:(at + 1) * sketch // 2, :] = unpack_signs(words_in[at, source])

    load_rank_words.wait()
    signs = unpack_signs(rank_words[...])
    sign_rank[...] = jnp.concatenate([signs, signs], axis=1)
    unpack_slice(x)
    load_act.wait()
    right[...] = lax.dot_general(
        act_in[x], sign_feat[...], NT, preferred_element_type=jnp.float32
    )

    def send_near(piece):
        return remote(
            near_out.at[piece], near_in.at[piece],
            near_send.at[piece], near_recv.at[piece], my_dp, x * NZ + near,
        )

    def send_far(piece):
        return remote(
            far_out.at[piece], far_in.at[piece],
            far_send.at[piece], far_recv.at[piece], my_dp, x * NZ + far,
        )

    for piece in range(NZ):
        total = part[x, piece].astype(jnp.float32)
        for source in ring_x:
            arrived(part_in.at[source, piece], part_recv.at[source, piece]).wait_recv()
            total = total + part_in[source, piece].astype(jnp.float32)
        rank_sum[piece] = total
        near_out[piece] = total.astype(jnp.bfloat16)
        send_near(piece).start()

    for source in ring_x:
        arrived(words_in.at[half, source], words_recv.at[source]).wait_recv()
        send_twin(source).start()

    for piece in range(NZ):
        arrived(near_in.at[piece], near_recv.at[piece]).wait_recv()
        total = rank_sum[piece] + near_in[piece].astype(jnp.float32)
        rank_sum[piece] = total
        far_out[piece] = total.astype(jnp.bfloat16)
        send_far(piece).start()

    @pl.when(z == 0)
    def _():
        for to in dp_peers:
            pl.semaphore_signal(word_y, inc=1, device_id=(to, me), device_id_type=MESH)

    for source in ring_x[1:] + ring_x[:1]:
        arrived(words_in.at[1 - half, source], twin_recv.at[source]).wait_recv()
        unpack_slice(source)
        arrived(act_in.at[source], act_recv.at[source]).wait_recv()
        right[...] += lax.dot_general(
            act_in[source], sign_feat[...], NT, preferred_element_type=jnp.float32
        )

    load_lengths.wait()
    slot = lax.broadcasted_iota(jnp.int32, (seq, LANES), 0)

    def send_raw(to):
        return remote(
            raw.at[to], raw_in.at[z], raw_send.at[to], raw_recv.at[z], my_dp, x * NZ + to
        )

    for piece in range(NZ):
        arrived(far_in.at[piece], far_recv.at[piece]).wait_recv()
        total = rank_sum[piece] + far_in[piece].astype(jnp.float32)
        live = jnp.concatenate(
            [
                (slot < lengths[x * examples + piece * own + example]).astype(jnp.float32)
                for example in range(own)
            ]
        )
        total = total * live
        high = total.astype(jnp.bfloat16)
        low = (total - high.astype(jnp.float32)).astype(jnp.bfloat16)
        left = lax.dot_general(
            jnp.concatenate([high, low], axis=1), sign_rank[...], NT,
            preferred_element_type=jnp.float32,
        )
        product = left * right[piece * rows:(piece + 1) * rows, :]
        sums = product.reshape(own, seq, sketch).sum(axis=1)
        for example in range(own):
            for block in range(blocks):
                line = example * blocks + block
                raw[piece, line:line + 1, :] = sums[
                    example:example + 1, block * LANES:(block + 1) * LANES
                ]

        @pl.when(z != piece)
        def _():
            send_raw(piece).start()

    @pl.when(z == 0)
    def _():
        pl.semaphore_wait(word_y, len(dp_peers))
        for to in ring_z:
            pl.semaphore_signal(
                word_z, inc=1, device_id=(my_dp, x * NZ + to), device_id_type=MESH
            )

    raw_sum = raw[z]
    for source in ring_z:
        arrived(raw_in.at[source], raw_recv.at[source]).wait_recv()
        raw_sum = raw_sum + raw_in[source]
    for example in range(own):
        lines = raw_sum[example * blocks:(example + 1) * blocks, :]
        mean = jnp.sum(lines * lines, keepdims=True) / sketch
        mine[example * blocks:(example + 1) * blocks, :] = lines * lax.rsqrt(mean + 1e-06)
    @pl.when(z != 0)
    def _():
        pl.semaphore_wait(word_z, 1)

    group[me] = mine[...].astype(jnp.bfloat16)
    others[my_dp] = mine[...].astype(jnp.bfloat16)

    for at, to in enumerate(dp_peers):
        remote(
            others.at[my_dp], others.at[my_dp], other_send, other_recv, to, me
        ).start()
        if at < len(mp_peers):
            remote(
                group.at[me], group.at[me], group_send, group_recv, my_dp, mp_peers[at]
            ).start()

    sketch_out[...] = jnp.concatenate(
        [mine[pl.ds(block, own, stride=blocks), :] for block in range(blocks)], axis=1
    ).astype(jnp.bfloat16)

    for to in ring_x:
        for piece in range(NZ):
            send_part(to, piece).wait_send()
        send_words(to).wait_send()
        send_twin(to).wait_send()
        send_act(to).wait_send()
    for piece in range(NZ):
        send_near(piece).wait_send()
        send_far(piece).wait_send()
    for to in ring_z:
        send_raw(to).wait_send()
    remote(
        group.at[pl.ds(0, n_mp - 1)], group.at[pl.ds(0, n_mp - 1)], group_send, group_recv, my_dp, me
    ).wait()
    group_f[...] = group[...].astype(jnp.float32).reshape(n_mp * width, LANES)
    remote(
        others.at[pl.ds(0, n_dp - 1)], others.at[pl.ds(0, n_dp - 1)], other_send, other_recv, my_dp, me
    ).wait()
    others_f[...] = others[...].astype(jnp.float32).reshape(n_dp * width, LANES)

    for example in range(own):
        cosines = jnp.zeros((n_mp * own, n_dp), jnp.float32)
        for block in range(blocks):
            here = group_f[pl.ds(block, n_mp * own, stride=blocks), :].astype(jnp.bfloat16)
            there = others_f[pl.ds(example * blocks + block, n_dp, stride=width), :]
            cosines = cosines + lax.dot_general(
                here, there.astype(jnp.bfloat16), NT, preferred_element_type=jnp.float32
            )
        cos_out[:, example, :] = cosines / sketch


def solution(mesh):
    n_dp, n_mp = mesh.shape["dp"], mesh.shape["mp"]

    def per_device(activations, gradients, up_matrix, rank_words, feat_words, lengths):
        examples = lengths.shape[0]
        tokens, features = activations.shape
        seq = tokens // examples
        own = examples // n_mp
        rank = up_matrix.shape[1]
        sketch = 16 * rank_words.shape[0]
        width = own * sketch // LANES
        quarter = tokens // NX
        pieces = (NX, NZ, own * seq, rank)
        bf16, f32, dma = jnp.bfloat16, jnp.float32, pltpu.SemaphoreType.DMA
        in_hbm = pl.BlockSpec(memory_space=pltpu.HBM)
        sketches, cosines = pl.pallas_call(
            functools.partial(kernel, n_dp, n_mp, seq),
            out_shape=[
                pltpu.VMEM((own, sketch), bf16),
                pltpu.VMEM((examples, own, n_dp), f32),
            ],
            in_specs=[in_hbm] * 6,
            out_specs=[pl.BlockSpec(memory_space=pltpu.VMEM)] * 2,
            scratch_shapes=[
                pltpu.VMEM((tokens, features), bf16),
                pltpu.VMEM((features, rank), bf16),
                pltpu.VMEM(rank_words.shape, jnp.int32),
                pltpu.VMEM(feat_words.shape, jnp.int32),
                pltpu.SMEM((examples,), jnp.int32),
                dma(()),
                dma(()),
                dma(()),
                dma(()),
                dma(()),
                pltpu.VMEM((NX, quarter, features), bf16),
                pltpu.VMEM((2, NX, feat_words.shape[0] // 2, features), jnp.int16),
                pltpu.VMEM(pieces, bf16),
                pltpu.VMEM(pieces, bf16),
                pltpu.VMEM(pieces[1:], f32),
                pltpu.VMEM(pieces[1:], bf16),
                pltpu.VMEM(pieces[1:], bf16),
                pltpu.VMEM(pieces[1:], bf16),
                pltpu.VMEM(pieces[1:], bf16),
                pltpu.VMEM((sketch, 2 * rank), bf16),
                pltpu.VMEM((sketch, features), bf16),
                pltpu.VMEM((quarter, sketch), f32),
                pltpu.VMEM((NZ, width, LANES), f32),
                pltpu.VMEM((NZ, width, LANES), f32),
                pltpu.VMEM((width, LANES), f32),
                pltpu.VMEM((n_mp, width, LANES), bf16),
                pltpu.VMEM((n_dp, width, LANES), bf16),
                pltpu.VMEM((n_mp * width, LANES), f32),
                pltpu.VMEM((n_dp * width, LANES), f32),
            ]
            + [dma((NX,))] * 6
            + [dma((NX, NZ))] * 2
            + [dma((NZ,))] * 6
            + [dma(())] * 4
            + [pltpu.SemaphoreType.REGULAR] * 2,
            compiler_params=pltpu.CompilerParams(
                collective_id=0, has_side_effects=True, vmem_limit_bytes=48 * 1024 * 1024
            ),
        )(*[pltpu.with_memory_space_constraint(each, pltpu.HBM) for each in (activations, gradients, up_matrix, rank_words, feat_words, lengths)])
        return sketches, cosines.transpose(0, 2, 1)

    return jax.shard_map(
        per_device,
        mesh=mesh,
        in_specs=(P("dp", "mp"), P("dp", "mp"), P("mp", None), P(), P(None, "mp"), P("dp")),
        out_specs=(P(("dp", "mp"), None), P("dp", None, "mp")),
        check_vma=False,
    )
```

```python
import functools

import jax
import jax.numpy as jnp
from jax import lax
from jax.experimental import pallas as pl
from jax.experimental.pallas import tpu as pltpu
from jax.sharding import PartitionSpec as P

MESH = pl.DeviceIdType.MESH
NT = (((1,), (1,)), ((), ()))
LANES = 128
NX, NZ = 4, 4
DIRECT = (0, NZ - 1)
NY, NC = 8, 4


def far_first(count):
    return sorted(range(1, count), key=lambda step: -min(step, count - step))


def unpack_signs(words):
    words = words.astype(jnp.int32)
    shape = (words.shape[0], 16, words.shape[1])
    offsets = lax.broadcasted_iota(jnp.int32, shape, 1)
    bits = jnp.bitwise_and(jnp.right_shift(words[:, None, :], offsets), 1)
    signs = (2 * bits - 1).astype(jnp.float32).astype(jnp.bfloat16)
    return signs.reshape(shape[0] * 16, shape[2])


def kernel(
    n_dp, n_mp, seq,
    act_hbm, grad_hbm, up_hbm, rank_words_hbm, feat_words_hbm, lengths_hbm,
    sketch_out, cos_out,
    grad, up, rank_words, feat_words, lengths,
    up_sem, grad_sem, rank_words_sem, feat_words_sem, lengths_sem,
    act_own, act_own_sem, act_in, words_in, part, part_in, rank_sum, near_out, near_in, far_out, far_in, opposite_in,
    sign_rank, sign_feat, right,
    raw, raw_in, mine, group, others, group_f, others_f,
    act_send, act_recv, words_send, words_recv, twin_send, twin_recv, part_send, part_recv,
    near_send, near_recv, far_send, far_recv, raw_send, raw_recv,
    group_send, group_recv, other_send, other_recv, opposite_send, opposite_recv, word_near, word_y, word_z,
):
    my_dp = lax.axis_index("dp")
    me = lax.axis_index("mp")
    x, z = me // NZ, me % NZ
    y, core = my_dp // NC, my_dp % NC
    rows = part.shape[2]
    quarter = NZ * rows
    own = rows // seq
    examples = NZ * own
    sketch = sign_feat.shape[1]
    blocks = sketch // LANES
    width = own * blocks
    ring_x = [(x + step) % NX for step in far_first(NX)]
    ring_z = [(z + step) % NZ for step in far_first(NZ)]
    ring_y = [(y + step) % NY for step in far_first(NY)]
    ring_c = [(core + step) % NC for step in range(1, NC)]
    mp_peers = [to_x * NZ + to_z for to_z in ring_z for to_x in ring_x + [x]]
    mp_peers += [to_x * NZ + z for to_x in ring_x]
    dp_peers = [to_y * NC + to_c for to_y in ring_y for to_c in ring_c + [core]]
    dp_peers += [y * NC + to_c for to_c in ring_c]

    def rows_of(ref, at):
        return ref.at[pl.ds(pl.multiple_of(at * quarter, quarter), quarter), :]

    def remote(src, dst, send_sem, recv_sem, to_dp, to_mp):
        return pltpu.make_async_remote_copy(
            src_ref=src, dst_ref=dst, send_sem=send_sem, recv_sem=recv_sem,
            device_id=(to_dp, to_mp), device_id_type=MESH,
        )

    def arrived(ref, sem):
        return remote(ref, ref, sem, sem, my_dp, me)

    half = my_dp % 2
    twin = my_dp + 1 - 2 * half
    near = z + 1 - 2 * (z % 2)
    far = NZ - 1 - z
    greeted = [(my_dp, to_x * NZ + z) for to_x in ring_x]
    greeted += [(my_dp, x * NZ + near), (my_dp, x * NZ + far), (twin, me)]
    barrier = pltpu.get_barrier_semaphore()
    for to in greeted:
        pl.semaphore_signal(barrier, inc=1, device_id=to, device_id_type=MESH)

    load_up = pltpu.make_async_copy(up_hbm, up, up_sem)
    load_grad = pltpu.make_async_copy(grad_hbm, grad, grad_sem)
    load_words = pltpu.make_async_copy(feat_words_hbm, feat_words, feat_words_sem)
    load_act = pltpu.make_async_copy(rows_of(act_hbm, x), act_own, act_own_sem)
    load_rank_words = pltpu.make_async_copy(rank_words_hbm, rank_words, rank_words_sem)
    load_lengths = pltpu.make_async_copy(lengths_hbm, lengths, lengths_sem)
    for load in (load_up, load_grad, load_words, load_act, load_rank_words, load_lengths):
        load.start()

    @pl.when(z == 0)
    def _():
        for to in dp_peers:
            pl.semaphore_signal(barrier, inc=1, device_id=(to, me), device_id_type=MESH)

    load_up.wait()
    load_grad.wait()
    for to in ring_x + [x]:
        tokens = grad[pl.ds(pl.multiple_of(to * quarter, quarter), quarter), :]
        part[to] = (
            jnp.dot(tokens, up[...], preferred_element_type=jnp.float32)
            .astype(jnp.bfloat16)
            .reshape(NZ, rows, LANES)
        )
    load_words.wait()
    half_words = feat_words.shape[0] // 2
    for at in range(2):
        words_in[at, x] = feat_words[at * half_words:(at + 1) * half_words, :].astype(jnp.int16)

    @pl.when(z == 0)
    def _():
        pl.semaphore_wait(barrier, len(greeted) + len(dp_peers))

    @pl.when(z != 0)
    def _():
        pl.semaphore_wait(barrier, len(greeted))

    def send_part(to, piece):
        return remote(
            part.at[to, piece], part_in.at[x, piece],
            part_send.at[to, piece], part_recv.at[x, piece], my_dp, to * NZ + z,
        )

    def send_words(to):
        return remote(
            words_in.at[half, x], words_in.at[half, x],
            words_send.at[to], words_recv.at[x], my_dp, to * NZ + z,
        )

    def send_twin(source):
        return remote(
            words_in.at[half, source], words_in.at[half, source],
            twin_send.at[source], twin_recv.at[source], twin, me,
        )

    def send_act(to, part_of):
        first = pl.multiple_of(to * quarter + part_of * quarter // 2, quarter // 2)
        return remote(
            act_hbm.at[pl.ds(first, quarter // 2), :], act_in.at[x, part_of],
            act_send.at[to, part_of], act_recv.at[x, part_of], my_dp, to * NZ + z,
        )

    for to in ring_x:
        send_part(to, 0).start()
    for to in ring_x:
        send_words(to).start()
    for piece in range(1, NZ):
        for to in ring_x:
            send_part(to, piece).start()
    for to in ring_x:
        send_act(to, 0).start()

    pl.semaphore_signal(word_near, inc=1, device_id=(my_dp, x * NZ + near), device_id_type=MESH)
    pl.semaphore_wait(word_near, 1)

    @pl.when(z == 0)
    def _():
        for to in dp_peers:
            pl.semaphore_signal(word_y, inc=1, device_id=(to, me), device_id_type=MESH)

    def unpack_slice(source):
        for at in range(2):
            sign_feat[source, at * sketch // 2:(at + 1) * sketch // 2, :] = unpack_signs(words_in[at, source])

    load_rank_words.wait()
    sign_rank[...] = unpack_signs(rank_words[...])
    unpack_slice(x)
    load_act.wait()
    right[...] = lax.dot_general(
        act_own[...], sign_feat[x], NT, preferred_element_type=jnp.float32
    )

    def send_near(piece):
        return remote(
            near_out.at[piece], near_in.at[piece],
            near_send.at[piece], near_recv.at[piece], my_dp, x * NZ + near,
        )

    def send_far(piece):
        return remote(
            (near_out if piece in DIRECT else far_out).at[piece], far_in.at[piece],
            far_send.at[piece], far_recv.at[piece], my_dp, x * NZ + far,
        )

    def send_opposite(piece):
        return remote(
            near_out.at[piece], opposite_in.at[piece],
            opposite_send.at[piece], opposite_recv.at[piece], my_dp, x * NZ + (z + NZ // 2) % NZ,
        )

    def sum_row(piece):
        total = part[x, piece].astype(jnp.float32)
        for source in ring_x:
            arrived(part_in.at[source, piece], part_recv.at[source, piece]).wait_recv()
            total = total + part_in[source, piece].astype(jnp.float32)
        rank_sum[piece] = total
        near_out[piece] = total.astype(jnp.bfloat16)
        if piece in DIRECT:
            send_opposite(piece).start()
            send_far(piece).start()
        send_near(piece).start()
    def add_near(piece):
        arrived(near_in.at[piece], near_recv.at[piece]).wait_recv()
        total = rank_sum[piece] + near_in[piece].astype(jnp.float32)
        rank_sum[piece] = total
        if piece not in DIRECT:
            far_out[piece] = total.astype(jnp.bfloat16)
            send_far(piece).start()

    def add_activations(part_of):
        at = slice(part_of * quarter // 2, (part_of + 1) * quarter // 2)
        right_sum = right[at, :]
        for source in ring_x:
            arrived(act_in.at[source, part_of], act_recv.at[source, part_of]).wait_recv()
            right_sum = right_sum + lax.dot_general(
                act_in[source, part_of], sign_feat[source], NT, preferred_element_type=jnp.float32
            )
        right[at, :] = right_sum

    sum_row(0)
    for source in ring_x:
        arrived(words_in.at[half, source], words_recv.at[source]).wait_recv()
        send_twin(source).start()
    sum_row(1)
    for to in ring_x:
        send_act(to, 1).start()
    for source in ring_x:
        arrived(words_in.at[1 - half, source], twin_recv.at[source]).wait_recv()
        unpack_slice(source)
    sum_row(2)
    sum_row(3)
    add_near(1)
    add_near(2)

    load_lengths.wait()
    slot = lax.broadcasted_iota(jnp.int32, (seq, LANES), 0)

    def send_raw(to):
        return remote(
            raw.at[to], raw_in.at[z], raw_send.at[to], raw_recv.at[z], my_dp, x * NZ + to
        )

    for piece in range(NZ):
        at = slice(piece * rows, (piece + 1) * rows)
        if piece % (NZ // 2) == 0:
            add_activations(piece // (NZ // 2))
        if piece in DIRECT:
            add_near(piece)
        arrived(far_in.at[piece], far_recv.at[piece]).wait_recv()
        total = rank_sum[piece] + far_in[piece].astype(jnp.float32)
        if piece in DIRECT:
            arrived(opposite_in.at[piece], opposite_recv.at[piece]).wait_recv()
            total = total + opposite_in[piece].astype(jnp.float32)
        live = jnp.concatenate(
            [
                (slot < lengths[x * examples + piece * own + example]).astype(jnp.float32)
                for example in range(own)
            ]
        )
        total = total * live
        high = total.astype(jnp.bfloat16)
        low = (total - high.astype(jnp.float32)).astype(jnp.bfloat16)
        pair = lax.dot_general(
            jnp.concatenate([high, low]), sign_rank[...], NT, preferred_element_type=jnp.float32
        )
        left = pair[:rows] + pair[rows:]
        product = left * right[at, :]
        sums = product.reshape(own, seq, sketch).sum(axis=1)
        for example in range(own):
            for block in range(blocks):
                line = example * blocks + block
                raw[piece, line:line + 1, :] = sums[
                    example:example + 1, block * LANES:(block + 1) * LANES
                ]

        @pl.when(z != piece)
        def _():
            send_raw(piece).start()

        if piece == 0:

            @pl.when(z == 0)
            def _():
                pl.semaphore_wait(word_y, len(dp_peers))
                for to in ring_z:
                    pl.semaphore_signal(
                        word_z, inc=1, device_id=(my_dp, x * NZ + to), device_id_type=MESH
                    )

    raw_sum = raw[z]
    for source in ring_z:
        arrived(raw_in.at[source], raw_recv.at[source]).wait_recv()
        raw_sum = raw_sum + raw_in[source]
    for example in range(own):
        lines = raw_sum[example * blocks:(example + 1) * blocks, :]
        mean = jnp.sum(lines * lines, keepdims=True) / sketch
        mine[example * blocks:(example + 1) * blocks, :] = lines * lax.rsqrt(mean + 1e-06)
    @pl.when(z != 0)
    def _():
        pl.semaphore_wait(word_z, 1)

    group[me] = mine[...].astype(jnp.bfloat16)
    others[my_dp] = mine[...].astype(jnp.bfloat16)

    for at, to in enumerate(dp_peers):
        remote(
            others.at[my_dp], others.at[my_dp], other_send, other_recv, to, me
        ).start()
        if at < len(mp_peers):
            remote(
                group.at[me], group.at[me], group_send, group_recv, my_dp, mp_peers[at]
            ).start()

    sketch_out[...] = jnp.concatenate(
        [mine[pl.ds(block, own, stride=blocks), :] for block in range(blocks)], axis=1
    ).astype(jnp.bfloat16)

    for to in ring_x:
        for piece in range(NZ):
            send_part(to, piece).wait_send()
        send_words(to).wait_send()
        send_twin(to).wait_send()
        for part_of in range(2):
            send_act(to, part_of).wait_send()
    for piece in DIRECT:
        send_opposite(piece).wait_send()
    for piece in range(NZ):
        send_near(piece).wait_send()
        send_far(piece).wait_send()
    for to in ring_z:
        send_raw(to).wait_send()
    remote(
        group.at[pl.ds(0, n_mp - 1)], group.at[pl.ds(0, n_mp - 1)], group_send, group_recv, my_dp, me
    ).wait()
    group_f[...] = group[...].astype(jnp.float32).reshape(n_mp * width, LANES)
    remote(
        others.at[pl.ds(0, n_dp - 1)], others.at[pl.ds(0, n_dp - 1)], other_send, other_recv, my_dp, me
    ).wait()
    others_f[...] = others[...].astype(jnp.float32).reshape(n_dp * width, LANES)

    for example in range(own):
        cosines = jnp.zeros((n_mp * own, n_dp), jnp.float32)
        for block in range(blocks):
            here = group_f[pl.ds(block, n_mp * own, stride=blocks), :].astype(jnp.bfloat16)
            there = others_f[pl.ds(example * blocks + block, n_dp, stride=width), :]
            cosines = cosines + lax.dot_general(
                here, there.astype(jnp.bfloat16), NT, preferred_element_type=jnp.float32
            )
        cos_out[:, example, :] = cosines / sketch


def hand_on(sketches, cosines, sketches_out, cosines_out, sketches_sem, cosines_sem):
    copies = [
        pltpu.make_async_copy(cosines, cosines_out, cosines_sem),
        pltpu.make_async_copy(sketches, sketches_out, sketches_sem),
    ]
    for copy in copies:
        copy.start()
    for copy in copies:
        copy.wait()


def solution(mesh):
    n_dp, n_mp = mesh.shape["dp"], mesh.shape["mp"]

    def per_device(activations, gradients, up_matrix, rank_words, feat_words, lengths):
        examples = lengths.shape[0]
        tokens, features = activations.shape
        seq = tokens // examples
        own = examples // n_mp
        rank = up_matrix.shape[1]
        sketch = 16 * rank_words.shape[0]
        width = own * sketch // LANES
        quarter = tokens // NX
        pieces = (NX, NZ, own * seq, rank)
        bf16, f32, dma = jnp.bfloat16, jnp.float32, pltpu.SemaphoreType.DMA
        in_hbm = pl.BlockSpec(memory_space=pltpu.HBM)
        sketches, cosines = pl.pallas_call(
            functools.partial(kernel, n_dp, n_mp, seq),
            out_shape=[
                pltpu.VMEM((own, sketch), bf16),
                pltpu.VMEM((examples, own, n_dp), f32),
            ],
            in_specs=[in_hbm] * 6,
            out_specs=[pl.BlockSpec(memory_space=pltpu.VMEM)] * 2,
            scratch_shapes=[
                pltpu.VMEM((tokens, features), bf16),
                pltpu.VMEM((features, rank), bf16),
                pltpu.VMEM(rank_words.shape, jnp.int32),
                pltpu.VMEM(feat_words.shape, jnp.int32),
                pltpu.SMEM((examples,), jnp.int32),
                dma(()),
                dma(()),
                dma(()),
                dma(()),
                dma(()),
                pltpu.VMEM((quarter, features), bf16),
                dma(()),
                pltpu.VMEM((NX, 2, quarter // 2, features), bf16),
                pltpu.VMEM((2, NX, feat_words.shape[0] // 2, features), jnp.int16),
                pltpu.VMEM(pieces, bf16),
                pltpu.VMEM(pieces, bf16),
                pltpu.VMEM(pieces[1:], f32),
                pltpu.VMEM(pieces[1:], bf16),
                pltpu.VMEM(pieces[1:], bf16),
                pltpu.VMEM(pieces[1:], bf16),
                pltpu.VMEM(pieces[1:], bf16),
                pltpu.VMEM(pieces[1:], bf16),
                pltpu.VMEM((sketch, rank), bf16),
                pltpu.VMEM((NX, sketch, features), bf16),
                pltpu.VMEM((quarter, sketch), f32),
                pltpu.VMEM((NZ, width, LANES), f32),
                pltpu.VMEM((NZ, width, LANES), f32),
                pltpu.VMEM((width, LANES), f32),
                pltpu.VMEM((n_mp, width, LANES), bf16),
                pltpu.VMEM((n_dp, width, LANES), bf16),
                pltpu.VMEM((n_mp * width, LANES), f32),
                pltpu.VMEM((n_dp * width, LANES), f32),
            ]
            + [dma((NX, 2))] * 2
            + [dma((NX,))] * 4
            + [dma((NX, NZ))] * 2
            + [dma((NZ,))] * 6
            + [dma(())] * 4
            + [dma((NZ,))] * 2
            + [pltpu.SemaphoreType.REGULAR] * 3,
            compiler_params=pltpu.CompilerParams(
                collective_id=0, has_side_effects=True, vmem_limit_bytes=48 * 1024 * 1024
            ),
        )(*[pltpu.with_memory_space_constraint(each, pltpu.HBM) for each in (activations, gradients, up_matrix, rank_words, feat_words, lengths)])
        in_vmem = pl.BlockSpec(memory_space=pltpu.VMEM)
        sketches, cosines = pl.pallas_call(
            hand_on,
            out_shape=[
                jax.ShapeDtypeStruct(sketches.shape, bf16),
                jax.ShapeDtypeStruct(cosines.shape, f32),
            ],
            in_specs=[in_vmem] * 2,
            out_specs=[in_hbm] * 2,
            scratch_shapes=[dma(()), dma(())],
        )(
            pltpu.with_memory_space_constraint(sketches, pltpu.VMEM),
            pltpu.with_memory_space_constraint(cosines, pltpu.VMEM),
        )
        return sketches, cosines.transpose(0, 2, 1)

    return jax.shard_map(
        per_device,
        mesh=mesh,
        in_specs=(P("dp", "mp"), P("dp", "mp"), P("mp", None), P(), P(None, "mp"), P("dp")),
        out_specs=(P(("dp", "mp"), None), P("dp", None, "mp")),
        check_vma=False,
    )
```

```python
import functools

import jax
import jax.numpy as jnp
from jax import lax
from jax.experimental import pallas as pl
from jax.experimental.pallas import tpu as pltpu
from jax.sharding import PartitionSpec as P

MESH = pl.DeviceIdType.MESH
NT = (((1,), (1,)), ((), ()))
LANES = 128
NX, NZ = 4, 4
NY, NC = 8, 4


def far_first(count):
    return sorted(range(1, count), key=lambda step: -min(step, count - step))


def unpack_signs(words):
    words = words.astype(jnp.int32)
    shape = (words.shape[0], 16, words.shape[1])
    offsets = lax.broadcasted_iota(jnp.int32, shape, 1)
    bits = jnp.bitwise_and(jnp.right_shift(words[:, None, :], offsets), 1)
    signs = (2 * bits - 1).astype(jnp.float32).astype(jnp.bfloat16)
    return signs.reshape(shape[0] * 16, shape[2])


def kernel(
    n_dp, n_mp, seq,
    act_hbm, grad_hbm, up_hbm, rank_words_hbm, feat_words_hbm, lengths_hbm,
    sketch_out, cos_out,
    grad, up, rank_words, feat_words, lengths,
    up_sem, grad_sem, rank_words_sem, feat_words_sem, lengths_sem,
    act_own, act_own_sem, act_in, words_in, part, part_in, rank_sum, rank_out, rank_in,
    sign_rank, sign_feat, right,
    raw_in, mine, group, others, group_f, others_f,
    act_send, act_recv, words_send, words_recv, twin_send, twin_recv, part_send, part_recv,
    rank_send, rank_recv, raw_send, raw_recv,
    group_send, group_recv, other_send, other_recv, word_near, word_y, word_z,
):
    my_dp = lax.axis_index("dp")
    me = lax.axis_index("mp")
    x, z = me // NZ, me % NZ
    y, core = my_dp // NC, my_dp % NC
    rows = part.shape[2]
    quarter = NZ * rows
    own = rows // seq
    examples = NZ * own
    sketch = sign_feat.shape[1]
    blocks = sketch // LANES
    width = own * blocks
    ring_x = [(x + step) % NX for step in far_first(NX)]
    ring_z = [(z + step) % NZ for step in far_first(NZ)]
    ring_y = [(y + step) % NY for step in far_first(NY)]
    ring_c = [(core + step) % NC for step in range(1, NC)]
    dp_peers = [to_y * NC + to_c for to_y in ring_y for to_c in ring_c + [core]]
    dp_peers += [y * NC + to_c for to_c in ring_c]

    def rows_of(ref, at):
        return ref.at[pl.ds(pl.multiple_of(at * quarter, quarter), quarter), :]

    def remote(src, dst, send_sem, recv_sem, to_dp, to_mp):
        return pltpu.make_async_remote_copy(
            src_ref=src, dst_ref=dst, send_sem=send_sem, recv_sem=recv_sem,
            device_id=(to_dp, to_mp), device_id_type=MESH,
        )

    def arrived(ref, sem):
        return remote(ref, ref, sem, sem, my_dp, me)

    half = my_dp % 2
    twin = my_dp + 1 - 2 * half
    near = z + 1 - 2 * (z % 2)
    far = NZ - 1 - z
    greeted = [(my_dp, to_x * NZ + z) for to_x in ring_x]
    greeted += [(my_dp, x * NZ + near), (my_dp, x * NZ + far), (twin, me)]
    barrier = pltpu.get_barrier_semaphore()
    for to in greeted:
        pl.semaphore_signal(barrier, inc=1, device_id=to, device_id_type=MESH)

    load_up = pltpu.make_async_copy(up_hbm, up, up_sem)
    load_grad = pltpu.make_async_copy(grad_hbm, grad, grad_sem)
    load_words = pltpu.make_async_copy(feat_words_hbm, feat_words, feat_words_sem)
    load_act = pltpu.make_async_copy(rows_of(act_hbm, x), act_own, act_own_sem)
    load_rank_words = pltpu.make_async_copy(rank_words_hbm, rank_words, rank_words_sem)
    load_lengths = pltpu.make_async_copy(lengths_hbm, lengths, lengths_sem)
    for load in (load_up, load_grad, load_words, load_act, load_rank_words, load_lengths):
        load.start()

    @pl.when(z == 0)
    def _():
        for to in dp_peers:
            pl.semaphore_signal(barrier, inc=1, device_id=(to, me), device_id_type=MESH)

    load_up.wait()
    load_grad.wait()
    for to in ring_x + [x]:
        tokens = grad[pl.ds(pl.multiple_of(to * quarter, quarter), quarter), :]
        part[to] = (
            jnp.dot(tokens, up[...], preferred_element_type=jnp.float32)
            .astype(jnp.bfloat16)
            .reshape(NZ, rows, LANES)
        )
    load_words.wait()
    half_words = feat_words.shape[0] // 2
    for at in range(2):
        words_in[at, x] = feat_words[at * half_words:(at + 1) * half_words, :].astype(jnp.int16)

    @pl.when(z == 0)
    def _():
        pl.semaphore_wait(barrier, len(greeted) + len(dp_peers))

    @pl.when(z != 0)
    def _():
        pl.semaphore_wait(barrier, len(greeted))

    def send_part(to, piece):
        return remote(
            part.at[to, piece], part_in.at[x, piece],
            part_send.at[to, piece], part_recv.at[x, piece], my_dp, to * NZ + z,
        )

    def send_words(to):
        return remote(
            words_in.at[half, x], words_in.at[half, x],
            words_send.at[to], words_recv.at[x], my_dp, to * NZ + z,
        )

    def send_twin(source):
        return remote(
            words_in.at[half, source], words_in.at[half, source],
            twin_send.at[source], twin_recv.at[source], twin, me,
        )

    def send_act(to, part_of):
        first = pl.multiple_of(to * quarter + part_of * quarter // 2, quarter // 2)
        return remote(
            act_hbm.at[pl.ds(first, quarter // 2), :], act_in.at[x, part_of],
            act_send.at[to, part_of], act_recv.at[x, part_of], my_dp, to * NZ + z,
        )

    for to in ring_x:
        send_part(to, 0).start()
    for to in ring_x:
        send_words(to).start()
    for piece in range(1, NZ):
        for to in ring_x:
            send_part(to, piece).start()

    pl.semaphore_signal(word_near, inc=1, device_id=(my_dp, x * NZ + near), device_id_type=MESH)

    def unpack_slice(source):
        for at in range(2):
            sign_feat[source, at * sketch // 2:(at + 1) * sketch // 2, :] = unpack_signs(words_in[at, source])

    load_rank_words.wait()
    sign_rank[...] = unpack_signs(rank_words[...])
    unpack_slice(x)
    load_act.wait()
    right[...] = lax.dot_general(
        act_own[...], sign_feat[x], NT, preferred_element_type=jnp.float32
    )

    def send_rank(to, piece):
        return remote(
            rank_out.at[piece], rank_in.at[z, piece],
            rank_send.at[to, piece], rank_recv.at[z, piece], my_dp, x * NZ + to,
        )

    def sum_row(piece):
        total = part[x, piece].astype(jnp.float32)
        for source in ring_x:
            arrived(part_in.at[source, piece], part_recv.at[source, piece]).wait_recv()
            total = total + part_in[source, piece].astype(jnp.float32)
        rank_sum[piece] = total
        rank_out[piece] = total.astype(jnp.bfloat16)
        for to in ring_z:
            send_rank(to, piece).start()

    def add_activations(part_of):
        at = slice(part_of * quarter // 2, (part_of + 1) * quarter // 2)
        right_sum = right[at, :]
        for source in ring_x:
            arrived(act_in.at[source, part_of], act_recv.at[source, part_of]).wait_recv()
            right_sum = right_sum + lax.dot_general(
                act_in[source, part_of], sign_feat[source], NT, preferred_element_type=jnp.float32
            )
        right[at, :] = right_sum

    pl.semaphore_wait(word_near, 1)
    sum_row(0)
    for to in ring_x:
        send_act(to, 0).start()

    @pl.when(z == 0)
    def _():
        for to in dp_peers:
            pl.semaphore_signal(word_y, inc=1, device_id=(to, me), device_id_type=MESH)

    for source in ring_x:
        arrived(words_in.at[half, source], words_recv.at[source]).wait_recv()
        send_twin(source).start()
    sum_row(1)
    for to in ring_x:
        send_act(to, 1).start()
    for source in ring_x:
        arrived(words_in.at[1 - half, source], twin_recv.at[source]).wait_recv()
        unpack_slice(source)
    sum_row(2)
    sum_row(3)

    load_lengths.wait()
    slot = lax.broadcasted_iota(jnp.int32, (seq, LANES), 0)

    def send_raw(to, piece):
        return remote(
            raw_in.at[z, piece], raw_in.at[z, piece],
            raw_send.at[to, piece], raw_recv.at[z, piece], my_dp, x * NZ + to,
        )

    for piece in range(NZ):
        at = slice(piece * rows, (piece + 1) * rows)
        if piece % (NZ // 2) == 0:
            add_activations(piece // (NZ // 2))
        total = rank_sum[piece]
        for source in ring_z:
            arrived(rank_in.at[source, piece], rank_recv.at[source, piece]).wait_recv()
            total = total + rank_in[source, piece].astype(jnp.float32)
        live = jnp.concatenate(
            [
                (slot < lengths[x * examples + piece * own + example]).astype(jnp.float32)
                for example in range(own)
            ]
        )
        total = total * live
        high = total.astype(jnp.bfloat16)
        low = (total - high.astype(jnp.float32)).astype(jnp.bfloat16)
        pair = lax.dot_general(
            jnp.concatenate([high, low]), sign_rank[...], NT, preferred_element_type=jnp.float32
        )
        left = pair[:rows] + pair[rows:]
        product = left * right[at, :]
        sums = product.reshape(own, seq, sketch).sum(axis=1)
        for example in range(own):
            for block in range(blocks):
                line = example * blocks + block
                raw_in[z, piece, line:line + 1, :] = sums[
                    example:example + 1, block * LANES:(block + 1) * LANES
                ]

        for to in ring_z:
            send_raw(to, piece).start()

        if piece == 0:

            @pl.when(z == 0)
            def _():
                pl.semaphore_wait(word_y, len(dp_peers))
                for to in ring_z:
                    pl.semaphore_signal(
                        word_z, inc=1, device_id=(my_dp, x * NZ + to), device_id_type=MESH
                    )

    def unit_sketches(owner):
        for source in ring_z:
            arrived(raw_in.at[source, owner], raw_recv.at[source, owner]).wait_recv()
        total = raw_in[0, owner]
        for source in range(1, NZ):
            total = total + raw_in[source, owner]
        units = []
        for example in range(own):
            lines = total[example * blocks:(example + 1) * blocks, :]
            mean = jnp.sum(lines * lines, keepdims=True) / sketch
            units.append(lines * lax.rsqrt(mean + 1e-06))
        return jnp.concatenate(units)

    mine[...] = unit_sketches(z)

    @pl.when(z != 0)
    def _():
        pl.semaphore_wait(word_z, 1)

    group[me] = mine[...].astype(jnp.bfloat16)
    others[my_dp] = mine[...].astype(jnp.bfloat16)

    for to in dp_peers:
        remote(
            others.at[my_dp], others.at[my_dp], other_send, other_recv, to, me
        ).start()
    for owner in ring_z:
        group[x * NZ + owner] = unit_sketches(owner).astype(jnp.bfloat16)
    quarter_group = group.at[pl.ds(x * NZ, NZ)]
    for to in ring_x:
        remote(
            quarter_group, quarter_group, group_send, group_recv, my_dp, to * NZ + z
        ).start()

    sketch_out[...] = jnp.concatenate(
        [mine[pl.ds(block, own, stride=blocks), :] for block in range(blocks)], axis=1
    ).astype(jnp.bfloat16)

    for to in ring_x:
        for piece in range(NZ):
            send_part(to, piece).wait_send()
        send_words(to).wait_send()
        send_twin(to).wait_send()
        for part_of in range(2):
            send_act(to, part_of).wait_send()
    for to in ring_z:
        for piece in range(NZ):
            send_rank(to, piece).wait_send()
            send_raw(to, piece).wait_send()
    remote(
        group.at[pl.ds(0, n_mp - NZ)], group.at[pl.ds(0, n_mp - NZ)],
        group_send, group_recv, my_dp, me,
    ).wait()
    group_f[...] = group[...].astype(jnp.float32).reshape(n_mp * width, LANES)
    remote(
        others.at[pl.ds(0, n_dp - 1)], others.at[pl.ds(0, n_dp - 1)], other_send, other_recv, my_dp, me
    ).wait()
    others_f[...] = others[...].astype(jnp.float32).reshape(n_dp * width, LANES)

    for example in range(own):
        cosines = jnp.zeros((n_mp * own, n_dp), jnp.float32)
        for block in range(blocks):
            here = group_f[pl.ds(block, n_mp * own, stride=blocks), :].astype(jnp.bfloat16)
            there = others_f[pl.ds(example * blocks + block, n_dp, stride=width), :]
            cosines = cosines + lax.dot_general(
                here, there.astype(jnp.bfloat16), NT, preferred_element_type=jnp.float32
            )
        cos_out[:, example, :] = cosines / sketch


def hand_on(sketches, cosines, sketches_out, cosines_out, sketches_sem, cosines_sem):
    copies = [
        pltpu.make_async_copy(cosines, cosines_out, cosines_sem),
        pltpu.make_async_copy(sketches, sketches_out, sketches_sem),
    ]
    for copy in copies:
        copy.start()
    for copy in copies:
        copy.wait()


def solution(mesh):
    n_dp, n_mp = mesh.shape["dp"], mesh.shape["mp"]

    def per_device(activations, gradients, up_matrix, rank_words, feat_words, lengths):
        examples = lengths.shape[0]
        tokens, features = activations.shape
        seq = tokens // examples
        own = examples // n_mp
        rank = up_matrix.shape[1]
        sketch = 16 * rank_words.shape[0]
        width = own * sketch // LANES
        quarter = tokens // NX
        pieces = (NX, NZ, own * seq, rank)
        bf16, f32, dma = jnp.bfloat16, jnp.float32, pltpu.SemaphoreType.DMA
        in_hbm = pl.BlockSpec(memory_space=pltpu.HBM)
        sketches, cosines = pl.pallas_call(
            functools.partial(kernel, n_dp, n_mp, seq),
            out_shape=[
                pltpu.VMEM((own, sketch), bf16),
                pltpu.VMEM((examples, own, n_dp), f32),
            ],
            in_specs=[in_hbm] * 6,
            out_specs=[pl.BlockSpec(memory_space=pltpu.VMEM)] * 2,
            scratch_shapes=[
                pltpu.VMEM((tokens, features), bf16),
                pltpu.VMEM((features, rank), bf16),
                pltpu.VMEM(rank_words.shape, jnp.int32),
                pltpu.VMEM(feat_words.shape, jnp.int32),
                pltpu.SMEM((examples,), jnp.int32),
                dma(()),
                dma(()),
                dma(()),
                dma(()),
                dma(()),
                pltpu.VMEM((quarter, features), bf16),
                dma(()),
                pltpu.VMEM((NX, 2, quarter // 2, features), bf16),
                pltpu.VMEM((2, NX, feat_words.shape[0] // 2, features), jnp.int16),
                pltpu.VMEM(pieces, bf16),
                pltpu.VMEM(pieces, bf16),
                pltpu.VMEM(pieces[1:], f32),
                pltpu.VMEM(pieces[1:], bf16),
                pltpu.VMEM((NZ,) + pieces[1:], bf16),
                pltpu.VMEM((sketch, rank), bf16),
                pltpu.VMEM((NX, sketch, features), bf16),
                pltpu.VMEM((quarter, sketch), f32),
                pltpu.VMEM((NZ, NZ, width, LANES), f32),
                pltpu.VMEM((width, LANES), f32),
                pltpu.VMEM((n_mp, width, LANES), bf16),
                pltpu.VMEM((n_dp, width, LANES), bf16),
                pltpu.VMEM((n_mp * width, LANES), f32),
                pltpu.VMEM((n_dp * width, LANES), f32),
            ]
            + [dma((NX, 2))] * 2
            + [dma((NX,))] * 4
            + [dma((NX, NZ))] * 2
            + [dma((NZ, NZ))] * 4
            + [dma(())] * 4
            + [pltpu.SemaphoreType.REGULAR] * 3,
            compiler_params=pltpu.CompilerParams(
                collective_id=0, has_side_effects=True, vmem_limit_bytes=48 * 1024 * 1024
            ),
        )(*[pltpu.with_memory_space_constraint(each, pltpu.HBM) for each in (activations, gradients, up_matrix, rank_words, feat_words, lengths)])
        in_vmem = pl.BlockSpec(memory_space=pltpu.VMEM)
        sketches, cosines = pl.pallas_call(
            hand_on,
            out_shape=[
                jax.ShapeDtypeStruct(sketches.shape, bf16),
                jax.ShapeDtypeStruct(cosines.shape, f32),
            ],
            in_specs=[in_vmem] * 2,
            out_specs=[in_hbm] * 2,
            scratch_shapes=[dma(()), dma(())],
        )(
            pltpu.with_memory_space_constraint(sketches, pltpu.VMEM),
            pltpu.with_memory_space_constraint(cosines, pltpu.VMEM),
        )
        return sketches, cosines.transpose(0, 2, 1)

    return jax.shard_map(
        per_device,
        mesh=mesh,
        in_specs=(P("dp", "mp"), P("dp", "mp"), P("mp", None), P(), P(None, "mp"), P("dp")),
        out_specs=(P(("dp", "mp"), None), P("dp", None, "mp")),
        check_vma=False,
    )
```

```python
import functools

import jax
import jax.numpy as jnp
from jax import lax
from jax.experimental import pallas as pl
from jax.experimental.pallas import tpu as pltpu
from jax.sharding import PartitionSpec as P

MESH = pl.DeviceIdType.MESH
NT = (((1,), (1,)), ((), ()))
LANES = 128
NX, NZ = 4, 4
NY, NC = 8, 4


def far_first(count):
    return sorted(range(1, count), key=lambda step: -min(step, count - step))


def unpack_signs(words):
    words = words.astype(jnp.int32)
    shape = (words.shape[0], 16, words.shape[1])
    offsets = lax.broadcasted_iota(jnp.int32, shape, 1)
    bits = jnp.bitwise_and(jnp.right_shift(words[:, None, :], offsets), 1)
    signs = (2 * bits - 1).astype(jnp.float32).astype(jnp.bfloat16)
    return signs.reshape(shape[0] * 16, shape[2])


def kernel(
    n_dp, n_mp, seq,
    act_hbm, grad_hbm, up_hbm, rank_words_hbm, feat_words_hbm, lengths_hbm,
    sketch_out, cos_out,
    grad, up, rank_words, feat_words, lengths,
    up_sem, grad_sem, rank_words_sem, feat_words_sem, lengths_sem,
    act_own, act_own_sem, act_in, words_in, part, part_in, rank_sum, rank_out, rank_in,
    sign_rank, sign_feat, right,
    raw_in, mine, group, others, group_f, others_f,
    act_send, act_recv, words_send, words_recv, twin_send, twin_recv, part_send, part_recv,
    rank_send, rank_recv, raw_send, raw_recv,
    group_send, group_recv, other_send, other_recv, word_near, word_y, word_z,
):
    my_dp = lax.axis_index("dp")
    me = lax.axis_index("mp")
    x, z = me // NZ, me % NZ
    y, core = my_dp // NC, my_dp % NC
    rows = part.shape[2]
    quarter = NZ * rows
    own = rows // seq
    examples = NZ * own
    sketch = sign_feat.shape[1]
    blocks = sketch // LANES
    width = own * blocks
    ring_x = [(x + step) % NX for step in far_first(NX)]
    ring_z = [(z + step) % NZ for step in far_first(NZ)]
    ring_y = [(y + step) % NY for step in far_first(NY)]
    ring_c = [(core + step) % NC for step in range(1, NC)]
    dp_peers = [to_y * NC + to_c for to_y in ring_y for to_c in ring_c + [core]]
    dp_peers += [y * NC + to_c for to_c in ring_c]

    def rows_of(ref, at):
        return ref.at[pl.ds(pl.multiple_of(at * quarter, quarter), quarter), :]

    def remote(src, dst, send_sem, recv_sem, to_dp, to_mp):
        return pltpu.make_async_remote_copy(
            src_ref=src, dst_ref=dst, send_sem=send_sem, recv_sem=recv_sem,
            device_id=(to_dp, to_mp), device_id_type=MESH,
        )

    def arrived(ref, sem):
        return remote(ref, ref, sem, sem, my_dp, me)

    half = my_dp % 2
    twin = my_dp + 1 - 2 * half
    near = z + 1 - 2 * (z % 2)
    far = NZ - 1 - z
    greeted = [(my_dp, to_x * NZ + z) for to_x in ring_x]
    greeted += [(my_dp, x * NZ + near), (my_dp, x * NZ + far), (twin, me)]
    barrier = pltpu.get_barrier_semaphore()
    for to in greeted:
        pl.semaphore_signal(barrier, inc=1, device_id=to, device_id_type=MESH)

    load_up = pltpu.make_async_copy(up_hbm, up, up_sem)
    load_grad = pltpu.make_async_copy(grad_hbm, grad, grad_sem)
    load_words = pltpu.make_async_copy(feat_words_hbm, feat_words, feat_words_sem)
    load_act = pltpu.make_async_copy(rows_of(act_hbm, x), act_own, act_own_sem)
    load_rank_words = pltpu.make_async_copy(rank_words_hbm, rank_words, rank_words_sem)
    load_lengths = pltpu.make_async_copy(lengths_hbm, lengths, lengths_sem)
    for load in (load_up, load_grad, load_words, load_act, load_rank_words, load_lengths):
        load.start()

    @pl.when(z == 0)
    def _():
        for to in dp_peers:
            pl.semaphore_signal(barrier, inc=1, device_id=(to, me), device_id_type=MESH)

    load_up.wait()
    load_grad.wait()
    for to in ring_x + [x]:
        tokens = grad[pl.ds(pl.multiple_of(to * quarter, quarter), quarter), :]
        part[to] = (
            jnp.dot(tokens, up[...], preferred_element_type=jnp.float32)
            .astype(jnp.bfloat16)
            .reshape(NZ, rows, LANES)
        )
    load_words.wait()
    half_words = feat_words.shape[0] // 2
    for at in range(2):
        words_in[at, x] = feat_words[at * half_words:(at + 1) * half_words, :].astype(jnp.int16)

    @pl.when(z == 0)
    def _():
        pl.semaphore_wait(barrier, len(greeted) + len(dp_peers))

    @pl.when(z != 0)
    def _():
        pl.semaphore_wait(barrier, len(greeted))

    def send_part(to, piece):
        return remote(
            part.at[to, piece], part_in.at[x, piece],
            part_send.at[to, piece], part_recv.at[x, piece], my_dp, to * NZ + z,
        )

    def send_words(to):
        return remote(
            words_in.at[half, x], words_in.at[half, x],
            words_send.at[to], words_recv.at[x], my_dp, to * NZ + z,
        )

    def send_twin(source):
        return remote(
            words_in.at[half, source], words_in.at[half, source],
            twin_send.at[source], twin_recv.at[source], twin, me,
        )

    def send_act(to, part_of):
        first = pl.multiple_of(to * quarter + part_of * quarter // 2, quarter // 2)
        return remote(
            act_hbm.at[pl.ds(first, quarter // 2), :], act_in.at[x, part_of],
            act_send.at[to, part_of], act_recv.at[x, part_of], my_dp, to * NZ + z,
        )

    for to in ring_x:
        send_part(to, 0).start()
    for to in ring_x:
        send_words(to).start()
    for piece in range(1, NZ):
        for to in ring_x:
            send_part(to, piece).start()

    pl.semaphore_signal(word_near, inc=1, device_id=(my_dp, x * NZ + near), device_id_type=MESH)

    def unpack_slice(source):
        for at in range(2):
            sign_feat[source, at * sketch // 2:(at + 1) * sketch // 2, :] = unpack_signs(words_in[at, source])

    load_rank_words.wait()
    sign_rank[...] = unpack_signs(rank_words[...])
    unpack_slice(x)
    load_act.wait()
    right[...] = lax.dot_general(
        act_own[...], sign_feat[x], NT, preferred_element_type=jnp.float32
    )

    def send_rank(to, piece):
        return remote(
            rank_out.at[piece], rank_in.at[z, piece],
            rank_send.at[to, piece], rank_recv.at[z, piece], my_dp, x * NZ + to,
        )

    def sum_row(piece):
        total = part[x, piece].astype(jnp.float32)
        for source in ring_x:
            arrived(part_in.at[source, piece], part_recv.at[source, piece]).wait_recv()
            total = total + part_in[source, piece].astype(jnp.float32)
        rank_sum[piece] = total
        rank_out[piece] = total.astype(jnp.bfloat16)
        for to in ring_z:
            send_rank(to, piece).start()

    def add_activations(part_of):
        at = slice(part_of * quarter // 2, (part_of + 1) * quarter // 2)
        right_sum = right[at, :]
        for source in ring_x:
            arrived(act_in.at[source, part_of], act_recv.at[source, part_of]).wait_recv()
            right_sum = right_sum + lax.dot_general(
                act_in[source, part_of], sign_feat[source], NT, preferred_element_type=jnp.float32
            )
        right[at, :] = right_sum

    pl.semaphore_wait(word_near, 1)
    sum_row(0)
    for to in ring_x:
        send_act(to, 0).start()

    @pl.when(z == 0)
    def _():
        for to in dp_peers:
            pl.semaphore_signal(word_y, inc=1, device_id=(to, me), device_id_type=MESH)

    for source in ring_x:
        arrived(words_in.at[half, source], words_recv.at[source]).wait_recv()
        send_twin(source).start()
    sum_row(1)
    for to in ring_x:
        send_act(to, 1).start()
    for source in ring_x:
        arrived(words_in.at[1 - half, source], twin_recv.at[source]).wait_recv()
        unpack_slice(source)
    sum_row(2)
    sum_row(3)

    load_lengths.wait()
    slot = lax.broadcasted_iota(jnp.int32, (seq, LANES), 0)

    def send_raw(to, piece):
        return remote(
            raw_in.at[z, piece], raw_in.at[z, piece],
            raw_send.at[to, piece], raw_recv.at[z, piece], my_dp, x * NZ + to,
        )

    for piece in range(NZ):
        at = slice(piece * rows, (piece + 1) * rows)
        if piece % (NZ // 2) == 0:
            add_activations(piece // (NZ // 2))
        total = rank_sum[piece]
        for source in ring_z:
            arrived(rank_in.at[source, piece], rank_recv.at[source, piece]).wait_recv()
            total = total + rank_in[source, piece].astype(jnp.float32)
        live = jnp.concatenate(
            [
                (slot < lengths[x * examples + piece * own + example]).astype(jnp.float32)
                for example in range(own)
            ]
        )
        total = total * live
        high = total.astype(jnp.bfloat16)
        low = (total - high.astype(jnp.float32)).astype(jnp.bfloat16)
        pair = lax.dot_general(
            jnp.concatenate([high, low]), sign_rank[...], NT, preferred_element_type=jnp.float32
        )
        left = pair[:rows] + pair[rows:]
        product = left * right[at, :]
        sums = product.reshape(own, seq, sketch).sum(axis=1)
        for example in range(own):
            for block in range(blocks):
                line = example * blocks + block
                raw_in[z, piece, line:line + 1, :] = sums[
                    example:example + 1, block * LANES:(block + 1) * LANES
                ]

        for to in ring_z:
            send_raw(to, piece).start()

        if piece == 0:

            @pl.when(z == 0)
            def _():
                pl.semaphore_wait(word_y, len(dp_peers))
                for to in ring_z:
                    pl.semaphore_signal(
                        word_z, inc=1, device_id=(my_dp, x * NZ + to), device_id_type=MESH
                    )

    def unit_sketches(owner):
        for source in ring_z:
            arrived(raw_in.at[source, owner], raw_recv.at[source, owner]).wait_recv()
        total = raw_in[0, owner]
        for source in range(1, NZ):
            total = total + raw_in[source, owner]
        units = []
        for example in range(own):
            lines = total[example * blocks:(example + 1) * blocks, :]
            mean = jnp.sum(lines * lines, keepdims=True) / sketch
            units.append(lines * lax.rsqrt(mean + 1e-06))
        return jnp.concatenate(units)

    mine[...] = unit_sketches(z)

    @pl.when(z != 0)
    def _():
        pl.semaphore_wait(word_z, 1)

    group[me] = mine[...].astype(jnp.bfloat16)
    others[my_dp] = mine[...].astype(jnp.bfloat16)

    for to in dp_peers:
        remote(
            others.at[my_dp], others.at[my_dp], other_send, other_recv, to, me
        ).start()
    def send_group(owner):
        for to in ring_x:
            ready = group.at[x * NZ + owner]
            remote(ready, ready, group_send, group_recv, my_dp, to * NZ + z).start()

    send_group(z)
    for owner in [(z + step) % NZ for step in range(1, NZ)]:
        group[x * NZ + owner] = unit_sketches(owner).astype(jnp.bfloat16)
        send_group(owner)

    sketch_out[...] = jnp.concatenate(
        [mine[pl.ds(block, own, stride=blocks), :] for block in range(blocks)], axis=1
    ).astype(jnp.bfloat16)

    for to in ring_x:
        for piece in range(NZ):
            send_part(to, piece).wait_send()
        send_words(to).wait_send()
        send_twin(to).wait_send()
        for part_of in range(2):
            send_act(to, part_of).wait_send()
    for to in ring_z:
        for piece in range(NZ):
            send_rank(to, piece).wait_send()
            send_raw(to, piece).wait_send()
    remote(
        group.at[pl.ds(0, n_mp - NZ)], group.at[pl.ds(0, n_mp - NZ)],
        group_send, group_recv, my_dp, me,
    ).wait()
    group_f[...] = group[...].astype(jnp.float32).reshape(n_mp * width, LANES)
    remote(
        others.at[pl.ds(0, n_dp - 1)], others.at[pl.ds(0, n_dp - 1)], other_send, other_recv, my_dp, me
    ).wait()
    others_f[...] = others[...].astype(jnp.float32).reshape(n_dp * width, LANES)

    for example in range(own):
        cosines = jnp.zeros((n_mp * own, n_dp), jnp.float32)
        for block in range(blocks):
            here = group_f[pl.ds(block, n_mp * own, stride=blocks), :].astype(jnp.bfloat16)
            there = others_f[pl.ds(example * blocks + block, n_dp, stride=width), :]
            cosines = cosines + lax.dot_general(
                here, there.astype(jnp.bfloat16), NT, preferred_element_type=jnp.float32
            )
        cos_out[:, example, :] = cosines / sketch


def hand_on(sketches, cosines, sketches_out, cosines_out, sketches_sem, cosines_sem):
    copies = [
        pltpu.make_async_copy(cosines, cosines_out, cosines_sem),
        pltpu.make_async_copy(sketches, sketches_out, sketches_sem),
    ]
    for copy in copies:
        copy.start()
    for copy in copies:
        copy.wait()


def solution(mesh):
    n_dp, n_mp = mesh.shape["dp"], mesh.shape["mp"]

    def per_device(activations, gradients, up_matrix, rank_words, feat_words, lengths):
        examples = lengths.shape[0]
        tokens, features = activations.shape
        seq = tokens // examples
        own = examples // n_mp
        rank = up_matrix.shape[1]
        sketch = 16 * rank_words.shape[0]
        width = own * sketch // LANES
        quarter = tokens // NX
        pieces = (NX, NZ, own * seq, rank)
        bf16, f32, dma = jnp.bfloat16, jnp.float32, pltpu.SemaphoreType.DMA
        in_hbm = pl.BlockSpec(memory_space=pltpu.HBM)
        sketches, cosines = pl.pallas_call(
            functools.partial(kernel, n_dp, n_mp, seq),
            out_shape=[
                pltpu.VMEM((own, sketch), bf16),
                pltpu.VMEM((examples, own, n_dp), f32),
            ],
            in_specs=[in_hbm] * 6,
            out_specs=[pl.BlockSpec(memory_space=pltpu.VMEM)] * 2,
            scratch_shapes=[
                pltpu.VMEM((tokens, features), bf16),
                pltpu.VMEM((features, rank), bf16),
                pltpu.VMEM(rank_words.shape, jnp.int32),
                pltpu.VMEM(feat_words.shape, jnp.int32),
                pltpu.SMEM((examples,), jnp.int32),
                dma(()),
                dma(()),
                dma(()),
                dma(()),
                dma(()),
                pltpu.VMEM((quarter, features), bf16),
                dma(()),
                pltpu.VMEM((NX, 2, quarter // 2, features), bf16),
                pltpu.VMEM((2, NX, feat_words.shape[0] // 2, features), jnp.int16),
                pltpu.VMEM(pieces, bf16),
                pltpu.VMEM(pieces, bf16),
                pltpu.VMEM(pieces[1:], f32),
                pltpu.VMEM(pieces[1:], bf16),
                pltpu.VMEM((NZ,) + pieces[1:], bf16),
                pltpu.VMEM((sketch, rank), bf16),
                pltpu.VMEM((NX, sketch, features), bf16),
                pltpu.VMEM((quarter, sketch), f32),
                pltpu.VMEM((NZ, NZ, width, LANES), f32),
                pltpu.VMEM((width, LANES), f32),
                pltpu.VMEM((n_mp, width, LANES), bf16),
                pltpu.VMEM((n_dp, width, LANES), bf16),
                pltpu.VMEM((n_mp * width, LANES), f32),
                pltpu.VMEM((n_dp * width, LANES), f32),
            ]
            + [dma((NX, 2))] * 2
            + [dma((NX,))] * 4
            + [dma((NX, NZ))] * 2
            + [dma((NZ, NZ))] * 4
            + [dma(())] * 4
            + [pltpu.SemaphoreType.REGULAR] * 3,
            compiler_params=pltpu.CompilerParams(
                collective_id=0, has_side_effects=True, vmem_limit_bytes=48 * 1024 * 1024
            ),
        )(*[pltpu.with_memory_space_constraint(each, pltpu.HBM) for each in (activations, gradients, up_matrix, rank_words, feat_words, lengths)])
        in_vmem = pl.BlockSpec(memory_space=pltpu.VMEM)
        sketches, cosines = pl.pallas_call(
            hand_on,
            out_shape=[
                jax.ShapeDtypeStruct(sketches.shape, bf16),
                jax.ShapeDtypeStruct(cosines.shape, f32),
            ],
            in_specs=[in_vmem] * 2,
            out_specs=[in_hbm] * 2,
            scratch_shapes=[dma(()), dma(())],
        )(
            pltpu.with_memory_space_constraint(sketches, pltpu.VMEM),
            pltpu.with_memory_space_constraint(cosines, pltpu.VMEM),
        )
        return sketches, cosines.transpose(0, 2, 1)

    return jax.shard_map(
        per_device,
        mesh=mesh,
        in_specs=(P("dp", "mp"), P("dp", "mp"), P("mp", None), P(), P(None, "mp"), P("dp")),
        out_specs=(P(("dp", "mp"), None), P("dp", None, "mp")),
        check_vma=False,
    )
```
